256 devices in a mesh: ctx: 64 (over y, z, core), head: 4 (over x).
Axes of the slice: x: 4, y: 4, z: 8, core: 2. Of those that a mesh axis runs over, the one named last changes fastest.
Arguments:
- queries: bfloat16 [32768, 4096], P('ctx', 'head'), may hold values from -25 to 25
- key_rows: bfloat16 [32768, 4096], P('ctx', 'head'), may hold values from -6 to 6
- value_rows: bfloat16 [32768, 4096], P('ctx', 'head'), may hold values from -6 to 6
- norm_gain: float32 [4096], P('head'), may hold values from 0.5 to 1.5
- cotangent: bfloat16 [32768, 4096], P('ctx', 'head'), may hold values from -6 to 6
Outputs:
- normed: bfloat16 [32768, 4096], P('ctx', 'head')
- grad_queries: bfloat16 [32768, 4096], P('ctx', 'head')
- grad_keys: bfloat16 [32768, 4096], P('ctx', 'head')
- grad_values: bfloat16 [32768, 4096], P('ctx', 'head')
The draws below stay inside these ranges and needn't reach their ends.
All inputs are finite; a program needn't handle non-finite values.
Results may differ from the reference program's by a relative error of at most 0.015.
Values may be sent and summed in bfloat16 or wider, within the bound.
A program may use at most 192 MiB of HBM per device.

```python
import jax
import jax.numpy as jnp
from jax import lax

HEADS = 32
DH = 128
TOK_DEV = 512
WIDTH = 4096
TOKENS = 32768


def draw_queries(key, part):
    key = jax.random.fold_in(key, 7)
    noise_key, head_key = jax.random.split(key)
    jitter = jnp.exp(jax.random.uniform(head_key, (HEADS,), jnp.float32, -0.3, 0.3))
    position = jnp.arange(HEADS).astype(jnp.float32) / (HEADS - 1)
    base = jnp.clip(jax.random.normal(noise_key, (TOKENS, WIDTH), jnp.float32), -6.0, 6.0)
    ramp = jnp.power(3.0, position)
    column_scale = jnp.repeat(ramp * jitter, DH)
    return (base * column_scale[None, :]).astype(jnp.bfloat16)


def steps_of(rng, extent, cuts, low, top_value):
    def one(dim, parts):
        steps = jax.random.uniform(jax.random.fold_in(jax.random.fold_in(rng, 6), dim), (parts,), jnp.float32, low / len(cuts), top_value / len(cuts))
        return jnp.repeat(jnp.exp(steps), extent[dim] // parts).reshape((-1,) + (1,) * (len(extent) - dim - 1))

    loudness = one(*cuts[0])
    for cut in cuts[1:]:
        loudness = loudness * one(*cut)
    return loudness


def centred(rng, extent, deviation, reach, cuts=(), held_as=jnp.bfloat16):
    drawn = jax.random.normal(rng, extent, jnp.float32) * deviation
    if len(cuts) > 0:
        drawn = steps_of(rng, extent, cuts, -0.22, 0.18) * drawn
    return jnp.clip(drawn, min=-reach, max=reach).astype(held_as)


def setup_inputs(seed: int = 0) -> dict:
    key_of = jax.random.split(jax.random.key(seed), 6)
    return {
        "queries": draw_queries(jax.random.fold_in(key_of[5], 71), 0),
        "key_rows": centred(key_of[1], (TOKENS, WIDTH), 1.0, 6.0, ((0, 64), (1, 4))),
        "value_rows": centred(key_of[2], (TOKENS, WIDTH), 1.0, 6.0, ((0, 64), (1, 4))),
        "norm_gain": jnp.clip(1.0 + 0.1 * jax.random.normal(key_of[3], (WIDTH,), jnp.float32), 0.5, 1.5),
        "cotangent": centred(key_of[4], (TOKENS, WIDTH), 1.0, 6.0, ((0, 64), (1, 4))),
    }


def split_heads(matrix):
    blocks = TOKENS // TOK_DEV
    return matrix.reshape(blocks, TOK_DEV, HEADS, DH).transpose(2, 0, 1, 3)

def join_heads(stacked):
    return stacked.transpose(1, 2, 0, 3).reshape(TOKENS, WIDTH)

def head_parts(query, keyset, valueset):
    query32 = query.astype(jnp.float32)
    key32 = keyset.astype(jnp.float32)
    value32 = valueset.astype(jnp.float32)
    causal = jnp.tril(jnp.ones((TOK_DEV, TOK_DEV), dtype=jnp.bool_))
    local_state = jnp.einsum('btd,bte->bde', key32, value32)
    running = jnp.cumsum(local_state, axis=0)
    prefix = jnp.concatenate([jnp.zeros_like(local_state[:1]), running[:-1]], axis=0)
    scores = jnp.einsum('btd,bsd->bts', query32, key32) / DH
    weights = jnp.where(causal[None], scores, jnp.float32(0.0)).astype(jnp.bfloat16)
    prefix_low = prefix.astype(jnp.bfloat16).astype(jnp.float32)
    return (query32, key32, value32, causal, weights, prefix_low)

def forward_head(operands):
    query32, key32, value32, causal, weights, prefix_low = head_parts(*operands)
    attended = jnp.einsum('bts,bse->bte', weights.astype(jnp.float32), value32)
    return attended + jnp.einsum('btd,bde->bte', query32, prefix_low) / DH

def backward_head(operands):
    query, keyset, valueset, grad_out = operands
    query32, key32, value32, causal, weights, prefix_low = head_parts(query, keyset, valueset)
    grad32 = grad_out.astype(jnp.float32)
    grad_state = jnp.einsum('btd,bte->bde', query32, grad32)
    later_sum = jnp.flip(jnp.cumsum(jnp.flip(grad_state, 0), axis=0), 0)
    suffix = jnp.concatenate([later_sum[1:], jnp.zeros_like(grad_state[:1])], axis=0)
    suffix_low = suffix.astype(jnp.bfloat16).astype(jnp.float32)
    grad_scores = jnp.einsum('bte,bse->bts', grad32, value32) / DH
    grad_weights = jnp.where(causal[None], grad_scores, jnp.float32(0.0)).astype(jnp.bfloat16).astype(jnp.float32)
    weights32 = weights.astype(jnp.float32)
    grad_query = jnp.einsum('bts,bsd->btd', grad_weights, key32) + jnp.einsum('bte,bde->btd', grad32, prefix_low) / DH
    grad_key = jnp.einsum('bts,btd->bsd', grad_weights, query32) + jnp.einsum('bse,bde->bsd', value32, suffix_low) / DH
    grad_value = jnp.einsum('bts,bte->bse', weights32, grad32) + jnp.einsum('bsd,bde->bse', key32, suffix_low) / DH
    return (grad_query.astype(jnp.bfloat16), grad_key.astype(jnp.bfloat16), grad_value.astype(jnp.bfloat16))

def reference(queries, key_rows, value_rows, norm_gain, cotangent):
    query_heads = split_heads(queries)
    key_heads = split_heads(key_rows)
    value_heads = split_heads(value_rows)
    attended = join_heads(lax.map(forward_head, (query_heads, key_heads, value_heads)))
    radius = jnp.sqrt(lax.optimization_barrier(jnp.sum(attended * attended, axis=1)) / WIDTH + 1e-06)
    normed = (norm_gain * attended / radius[:, None]).astype(jnp.bfloat16)
    scaled = norm_gain * cotangent.astype(jnp.float32)
    factor = lax.optimization_barrier(jnp.sum(attended * scaled, axis=1)) / (WIDTH * radius * radius)
    grad_out = ((scaled - attended * factor[:, None]) / radius[:, None]).astype(jnp.bfloat16)
    grad_heads = split_heads(grad_out)
    grad_query, grad_key, grad_value = lax.map(backward_head, (query_heads, key_heads, value_heads, grad_heads))
    return (normed, join_heads(grad_query), join_heads(grad_key), join_heads(grad_value))
```

```python
import functools

import jax
import jax.numpy as jnp
from jax import lax
from jax.experimental import pallas as pl
from jax.experimental.pallas import tpu as pltpu
from jax.sharding import PartitionSpec as P

MESH = pl.DeviceIdType.MESH
F32 = jnp.float32
BF16 = jnp.bfloat16
DH = 128
TOK = 512
HEADS = 8
WIDTH = HEADS * DH
HALF = HEADS // 2 * DH
NY, NZ, NX = 4, 8, 4
CHIPS = NY * NZ
PIECE = HALF // CHIPS
FULL_WIDTH = WIDTH * NX
CUT = TOK // 2


def far_first():
    def reach(offset):
        return min(offset[0], NY - offset[0]) + min(offset[1], NZ - offset[1])

    offsets = [(dy, dz) for dy in range(NY) for dz in range(NZ) if dy or dz]
    return sorted(offsets, key=lambda offset: -reach(offset))


def nn(a, b):
    return lax.dot_general(a, b, (((1,), (0,)), ((), ())), preferred_element_type=F32)


def nt(a, b):
    return lax.dot_general(a, b, (((1,), (1,)), ((), ())), preferred_element_type=F32)


def tn(a, b):
    return lax.dot_general(a, b, (((0,), (0,)), ((), ())), preferred_element_type=F32)


def await_bytes(ref, sem):
    pltpu.make_async_copy(ref, ref, sem).wait()


def kernel(
    q_hbm,
    k_hbm,
    v_hbm,
    gain_hbm,
    c_hbm,
    normed,
    grad_q,
    grad_k,
    grad_v,
    q,
    k,
    v,
    gain,
    c,
    q8,
    g,
    w,
    att,
    part_k,
    part_v,
    inv_ref,
    fac_ref,
    state_own,
    state_out,
    state_in,
    chip_sum,
    owned,
    scanned,
    chip_scan,
    scan_out,
    scan,
    stats,
    load_sem,
    send_sem,
    recv_sem,
):
    place = lax.axis_index("ctx")
    hx = lax.axis_index("head")
    chip = lax.div(place, 2)
    core = lax.rem(place, 2)
    chip_y = lax.div(chip, NZ)
    chip_z = lax.rem(chip, NZ)
    sibling = (chip * 2 + 1 - core, hx)

    def chip_at(dy, dz):
        return lax.rem(chip_y + dy, NY) * NZ + lax.rem(chip_z + dz, NZ)

    offsets = far_first()
    barrier = pltpu.get_barrier_semaphore()

    def greet(device):
        pl.semaphore_signal(barrier, inc=1, device_id=device, device_id_type=MESH)

    for dy, dz in offsets:
        greet((chip_at(dy, dz) * 2 + core, hx))
    for step in range(1, NX):
        greet((place, lax.rem(hx + step, NX)))
    greet(sibling)

    loads = [
        pltpu.make_async_copy(src, dst, load_sem.at[n])
        for n, (src, dst) in enumerate(
            [(k_hbm, k), (v_hbm, v), (q_hbm, q), (gain_hbm, gain), (c_hbm, c)]
        )
    ]
    for load in loads:
        load.start()

    def columns(h):
        return pl.ds(pl.multiple_of(h * DH, DH), DH)

    def rows_of(h):
        return pl.ds(pl.multiple_of(h * DH, DH), DH)

    theirs = pl.multiple_of((1 - core) * HALF, HALF)
    ours = pl.multiple_of(core * HALF, HALF)

    def send(src, dst, n, device):
        pltpu.make_async_remote_copy(
            src_ref=src,
            dst_ref=dst,
            send_sem=send_sem.at[n],
            recv_sem=recv_sem.at[n],
            device_id=device,
            device_id_type=MESH,
        ).start()

    def scan_begin(s, local_state, first):
        def give(i, carry):
            state_out[s, rows_of(i), :] = local_state((1 - core) * (HEADS // 2) + i).astype(BF16)
            return carry

        lax.fori_loop(0, HEADS // 2, give, 0)
        if first:
            pl.semaphore_wait(barrier, len(offsets) + NX)
        send(state_out.at[s], state_in.at[s], 4 * s, sibling)

        def keep(i, carry):
            state_own[s, rows_of(i), :] = local_state(core * (HEADS // 2) + i)
            return carry

        lax.fori_loop(0, HEADS // 2, keep, 0)
        await_bytes(state_in.at[s], recv_sem.at[4 * s])
        both = state_own[s] + state_in[s].astype(F32)
        chip_sum[s] = both.astype(BF16).reshape(CHIPS, PIECE, DH)
        for dy, dz in offsets:
            other = chip_at(dy, dz)
            send(chip_sum.at[s, other], owned.at[s, chip], 4 * s + 1, (other * 2 + core, hx))
        owned[s, chip] = chip_sum[s, chip]

    def scan_middle(s, backward):
        await_bytes(owned.at[s, pl.ds(0, CHIPS - 1)], recv_sem.at[4 * s + 1])
        total = jnp.zeros((PIECE, DH), F32)
        for n in range(CHIPS):
            one = CHIPS - 1 - n if backward else n
            scanned[s, one] = total.astype(BF16)
            total = total + owned[s, one].astype(F32)
        for dy, dz in offsets:
            other = chip_at(dy, dz)
            send(scanned.at[s, other], chip_scan.at[s, chip], 4 * s + 2, (other * 2 + core, hx))
        chip_scan[s, chip] = scanned[s, chip]

    def scan_end(s, backward, scale):
        await_bytes(chip_scan.at[s, pl.ds(0, CHIPS - 1)], recv_sem.at[4 * s + 2])
        ahead = chip_scan[s].astype(F32).reshape(HALF, DH)
        leads = core == (1 if backward else 0)
        give = ahead + jnp.where(leads, state_own[s], 0.0)
        scan_out[s] = (give * scale).astype(BF16)
        send(scan_out.at[s], scan.at[s, pl.ds(ours, HALF)], 4 * s + 3, sibling)
        keep = ahead + jnp.where(leads, 0.0, state_in[s].astype(F32))
        scan[s, pl.ds(ours, HALF), :] = (keep * scale).astype(BF16)
        await_bytes(scan_out.at[s], recv_sem.at[4 * s + 3])

    row_at = lax.broadcasted_iota(jnp.int32, (CUT, CUT), 0)
    col_at = lax.broadcasted_iota(jnp.int32, (CUT, CUT), 1)
    causal = col_at <= row_at

    def lower(scores):
        return jnp.where(causal, scores, 0.0).astype(BF16)

    loads[0].wait()
    loads[1].wait()
    scan_begin(0, lambda h: tn(k[:, columns(h)], v[:, columns(h)]), True)
    for load in loads[2:]:
        load.wait()

    def inside(h, carry):
        col = columns(h)
        q8_h = q[:, col] * jnp.asarray(1.0 / DH, BF16)
        q8[:, col] = q8_h
        k_h, v_h = k[:, col], v[:, col]
        w00 = lower(nt(q8_h[:CUT], k_h[:CUT]))
        w[h, :CUT, :CUT] = w00
        att[:CUT, col] = nn(w00, v_h[:CUT])
        w10 = nt(q8_h[CUT:], k_h[:CUT]).astype(BF16)
        w11 = lower(nt(q8_h[CUT:], k_h[CUT:]))
        w[h, CUT:, :CUT] = w10
        w[h, CUT:, CUT:] = w11
        att[CUT:, col] = nn(w10, v_h[:CUT]) + nn(w11, v_h[CUT:])
        return carry

    lax.fori_loop(0, HEADS // 2, inside, 0)
    scan_middle(0, False)
    lax.fori_loop(HEADS // 2, HEADS, inside, 0)
    scan_end(0, False, 1.0)

    def across(h, carry):
        col = columns(h)
        att[:, col] += nn(q8[:, col], scan[0, rows_of(h), :])
        return carry

    lax.fori_loop(0, HEADS, across, 0)

    def row_sums(b, carry):
        rows = pl.ds(pl.multiple_of(b * DH, DH), DH)
        squares = jnp.zeros((DH, DH), F32)
        inner = jnp.zeros((DH, DH), F32)
        for h in range(HEADS):
            col = slice(h * DH, (h + 1) * DH)
            a = att[rows, col]
            squares += a * a
            inner += a * (gain[:, col] * c[rows, col].astype(F32))
        stats[hx, 0:1, rows] = jnp.sum(squares.T, axis=0, keepdims=True)
        stats[hx, 1:2, rows] = jnp.sum(inner.T, axis=0, keepdims=True)
        return carry

    lax.fori_loop(0, TOK // DH, row_sums, 0)
    for step in range(1, NX):
        send(stats.at[hx], stats.at[hx], 8, (place, lax.rem(hx + step, NX)))
    await_bytes(stats.at[pl.ds(0, NX - 1)], recv_sem.at[8])
    sums = stats[0] + stats[1] + stats[2] + stats[3]
    mean_square = sums[0:1] * (1.0 / FULL_WIDTH) + 1e-6
    inverse = 1.0 / jnp.sqrt(mean_square)
    factor = sums[1:2] / (FULL_WIDTH * mean_square)
    for b in range(TOK // DH):
        rows = slice(b * DH, (b + 1) * DH)
        inv_ref[rows, :] = jnp.broadcast_to(inverse[:, rows], (DH, DH)).T
        fac_ref[rows, :] = jnp.broadcast_to(factor[:, rows], (DH, DH)).T

    def gradient_state(h):
        col = columns(h)
        scaled = gain[:, col] * c[:, col].astype(F32)
        g_h = ((scaled - att[:, col] * fac_ref[...]) * inv_ref[...]).astype(BF16)
        g[:, col] = g_h
        return tn(q[:, col], g_h)

    scan_begin(1, gradient_state, False)

    def inside_back(h, carry):
        col = columns(h)
        normed[:, col] = (gain[:, col] * att[:, col] * inv_ref[...]).astype(BF16)
        q_h, k_h, v_h, g_h = q[:, col], k[:, col], v[:, col], g[:, col]
        g8 = g_h * jnp.asarray(1.0 / DH, BF16)
        before = scan[0, rows_of(h), :]
        u00 = lower(nt(g8[:CUT], v_h[:CUT]))
        u10 = nt(g8[CUT:], v_h[:CUT]).astype(BF16)
        u11 = lower(nt(g8[CUT:], v_h[CUT:]))
        grad_q[:CUT, col] = (nn(u00, k_h[:CUT]) + nt(g8[:CUT], before)).astype(BF16)
        grad_q[CUT:, col] = (
            nn(u10, k_h[:CUT]) + nn(u11, k_h[CUT:]) + nt(g8[CUT:], before)
        ).astype(BF16)
        part_k[:CUT, col] = tn(u00, q_h[:CUT]) + tn(u10, q_h[CUT:])
        part_k[CUT:, col] = tn(u11, q_h[CUT:])
        part_v[:CUT, col] = tn(w[h, :CUT, :CUT], g_h[:CUT]) + tn(w[h, CUT:, :CUT], g_h[CUT:])
        part_v[CUT:, col] = tn(w[h, CUT:, CUT:], g_h[CUT:])
        return carry

    lax.fori_loop(0, HEADS // 2, inside_back, 0)
    scan_middle(1, True)
    lax.fori_loop(HEADS // 2, HEADS, inside_back, 0)
    scan_end(1, True, 1.0 / DH)

    def last(h, carry):
        col = columns(h)
        after = scan[1, rows_of(h), :]
        grad_k[:, col] = (part_k[:, col] + nt(v[:, col], after)).astype(BF16)
        grad_v[:, col] = (part_v[:, col] + nn(k[:, col], after)).astype(BF16)
        return carry

    lax.fori_loop(0, HEADS, last, 0)

    for s in range(2):
        await_bytes(state_out.at[s], send_sem.at[4 * s])
        await_bytes(chip_sum.at[s, pl.ds(0, CHIPS - 1)], send_sem.at[4 * s + 1])
        await_bytes(scanned.at[s, pl.ds(0, CHIPS - 1)], send_sem.at[4 * s + 2])
        await_bytes(scan_out.at[s], send_sem.at[4 * s + 3])
    await_bytes(stats.at[pl.ds(0, NX - 1)], send_sem.at[8])


def per_device(queries, key_rows, value_rows, norm_gain, cotangent):
    block = jax.ShapeDtypeStruct((TOK, WIDTH), BF16)
    held = pltpu.VMEM((TOK, WIDTH), BF16)
    held32 = pltpu.VMEM((TOK, WIDTH), F32)
    half = pltpu.VMEM((2, HALF, DH), BF16)
    pieces = pltpu.VMEM((2, CHIPS, PIECE, DH), BF16)
    return pl.pallas_call(
        kernel,
        out_shape=[block] * 4,
        in_specs=[pl.BlockSpec(memory_space=pltpu.HBM)] * 5,
        out_specs=[pl.BlockSpec(memory_space=pltpu.VMEM)] * 4,
        scratch_shapes=[
            held,
            held,
            held,
            pltpu.VMEM((1, WIDTH), F32),
            held,
            held,
            held,
            pltpu.VMEM((HEADS, TOK, TOK), BF16),
            held32,
            held32,
            held32,
            pltpu.VMEM((TOK, DH), F32),
            pltpu.VMEM((TOK, DH), F32),
            pltpu.VMEM((2, HALF, DH), F32),
            half,
            half,
            pieces,
            pieces,
            pieces,
            pieces,
            half,
            pltpu.VMEM((2, 2 * HALF, DH), BF16),
            pltpu.VMEM((NX, 2, TOK), F32),
            pltpu.SemaphoreType.DMA((5,)),
            pltpu.SemaphoreType.DMA((9,)),
            pltpu.SemaphoreType.DMA((9,)),
        ],
        compiler_params=pltpu.CompilerParams(
            collective_id=0, has_side_effects=True, vmem_limit_bytes=40 << 20
        ),
    )(queries, key_rows, value_rows, norm_gain.reshape(1, WIDTH), cotangent)


def solution(mesh):
    placed = (P("ctx", "head"), P("ctx", "head"), P("ctx", "head"), P("head"), P("ctx", "head"))
    return jax.shard_map(
        per_device,
        mesh=mesh,
        in_specs=placed,
        out_specs=(P("ctx", "head"), P("ctx", "head"), P("ctx", "head"), P("ctx", "head")),
        check_vma=False,
    )
```

```python
import functools

import jax
import jax.numpy as jnp
from jax import lax
from jax.experimental import pallas as pl
from jax.experimental.pallas import tpu as pltpu
from jax.sharding import PartitionSpec as P

MESH = pl.DeviceIdType.MESH
F32 = jnp.float32
BF16 = jnp.bfloat16
DH = 128
TOK = 512
HEADS = 8
WIDTH = HEADS * DH
HALF = HEADS // 2 * DH
NY, NZ, NX = 4, 8, 4
CHIPS = NY * NZ
PIECE = HALF // CHIPS
FULL_WIDTH = WIDTH * NX
CUT = TOK // 2


def far_first():
    def reach(offset):
        return min(offset[0], NY - offset[0]) + min(offset[1], NZ - offset[1])

    offsets = [(dy, dz) for dy in range(NY) for dz in range(NZ) if dy or dz]
    return sorted(offsets, key=lambda offset: -reach(offset))


def nn(a, b):
    return lax.dot_general(a, b, (((1,), (0,)), ((), ())), preferred_element_type=F32)


def nt(a, b):
    return lax.dot_general(a, b, (((1,), (1,)), ((), ())), preferred_element_type=F32)


def tn(a, b):
    return lax.dot_general(a, b, (((0,), (0,)), ((), ())), preferred_element_type=F32)


def await_bytes(ref, sem):
    pltpu.make_async_copy(ref, ref, sem).wait()


def kernel(
    q_hbm,
    k_hbm,
    v_hbm,
    gain_hbm,
    c_hbm,
    normed,
    grad_q,
    k,
    v,
    part_k,
    part_v,
    suffix,
    q,
    gain,
    c,
    q8,
    g,
    w,
    att,
    inv_ref,
    fac_ref,
    state_own,
    state_out,
    state_in,
    chip_sum,
    owned,
    scanned,
    chip_scan,
    scan_out,
    scan,
    stats,
    load_sem,
    send_sem,
    recv_sem,
):
    place = lax.axis_index("ctx")
    hx = lax.axis_index("head")
    chip = lax.div(place, 2)
    core = lax.rem(place, 2)
    chip_y = lax.div(chip, NZ)
    chip_z = lax.rem(chip, NZ)
    sibling = (chip * 2 + 1 - core, hx)

    def chip_at(dy, dz):
        return lax.rem(chip_y + dy, NY) * NZ + lax.rem(chip_z + dz, NZ)

    offsets = far_first()
    barrier = pltpu.get_barrier_semaphore()

    def greet(device):
        pl.semaphore_signal(barrier, inc=1, device_id=device, device_id_type=MESH)

    for dy, dz in offsets:
        greet((chip_at(dy, dz) * 2 + core, hx))
    for step in range(1, NX):
        greet((place, lax.rem(hx + step, NX)))
    greet(sibling)

    loads = [
        pltpu.make_async_copy(src, dst, load_sem.at[n])
        for n, (src, dst) in enumerate(
            [(k_hbm, k), (v_hbm, v), (q_hbm, q), (gain_hbm, gain), (c_hbm, c)]
        )
    ]
    for load in loads:
        load.start()

    def columns(h):
        return pl.ds(pl.multiple_of(h * DH, DH), DH)

    def rows_of(h):
        return pl.ds(pl.multiple_of(h * DH, DH), DH)

    theirs = pl.multiple_of((1 - core) * HALF, HALF)
    ours = pl.multiple_of(core * HALF, HALF)

    def send(src, dst, n, device):
        pltpu.make_async_remote_copy(
            src_ref=src,
            dst_ref=dst,
            send_sem=send_sem.at[n],
            recv_sem=recv_sem.at[n],
            device_id=device,
            device_id_type=MESH,
        ).start()

    def scan_begin(s, local_state, first):
        def give(i, carry):
            state_out[s, rows_of(i), :] = local_state((1 - core) * (HEADS // 2) + i).astype(BF16)
            return carry

        lax.fori_loop(0, HEADS // 2, give, 0)
        if first:
            pl.semaphore_wait(barrier, len(offsets) + NX)
        send(state_out.at[s], state_in.at[s], 4 * s, sibling)

        def keep(i, carry):
            state_own[s, rows_of(i), :] = local_state(core * (HEADS // 2) + i)
            return carry

        lax.fori_loop(0, HEADS // 2, keep, 0)
        await_bytes(state_in.at[s], recv_sem.at[4 * s])
        both = state_own[s] + state_in[s].astype(F32)
        chip_sum[s] = both.astype(BF16).reshape(CHIPS, PIECE, DH)
        for dy, dz in offsets:
            other = chip_at(dy, dz)
            send(chip_sum.at[s, other], owned.at[s, chip], 4 * s + 1, (other * 2 + core, hx))
        owned[s, chip] = chip_sum[s, chip]

    def scan_middle(s, backward):
        await_bytes(owned.at[s, pl.ds(0, CHIPS - 1)], recv_sem.at[4 * s + 1])
        total = jnp.zeros((PIECE, DH), F32)
        for n in range(CHIPS):
            one = CHIPS - 1 - n if backward else n
            scanned[s, one] = total.astype(BF16)
            total = total + owned[s, one].astype(F32)
        for dy, dz in offsets:
            other = chip_at(dy, dz)
            send(scanned.at[s, other], chip_scan.at[s, chip], 4 * s + 2, (other * 2 + core, hx))
        chip_scan[s, chip] = scanned[s, chip]

    def scan_end(s, backward, scale):
        await_bytes(chip_scan.at[s, pl.ds(0, CHIPS - 1)], recv_sem.at[4 * s + 2])
        ahead = chip_scan[s].astype(F32).reshape(HALF, DH)
        leads = core == (1 if backward else 0)
        give = ahead + jnp.where(leads, state_own[s], 0.0)
        scan_out[s] = (give * scale).astype(BF16)
        send(scan_out.at[s], scan.at[s, pl.ds(ours, HALF)], 4 * s + 3, sibling)
        keep = ahead + jnp.where(leads, 0.0, state_in[s].astype(F32))
        scan[s, pl.ds(ours, HALF), :] = (keep * scale).astype(BF16)
        await_bytes(scan_out.at[s], recv_sem.at[4 * s + 3])

    row_at = lax.broadcasted_iota(jnp.int32, (CUT, CUT), 0)
    col_at = lax.broadcasted_iota(jnp.int32, (CUT, CUT), 1)
    causal = col_at <= row_at

    def lower(scores):
        return jnp.where(causal, scores, 0.0).astype(BF16)

    loads[0].wait()
    loads[1].wait()
    scan_begin(0, lambda h: tn(k[:, columns(h)], v[:, columns(h)]), True)
    for load in loads[2:]:
        load.wait()

    def inside(h, carry):
        col = columns(h)
        q8_h = q[:, col] * jnp.asarray(1.0 / DH, BF16)
        q8[:, col] = q8_h
        k_h, v_h = k[:, col], v[:, col]
        w00 = lower(nt(q8_h[:CUT], k_h[:CUT]))
        w[h, :CUT, :CUT] = w00
        att[:CUT, col] = nn(w00, v_h[:CUT])
        w10 = nt(q8_h[CUT:], k_h[:CUT]).astype(BF16)
        w11 = lower(nt(q8_h[CUT:], k_h[CUT:]))
        w[h, CUT:, :CUT] = w10
        w[h, CUT:, CUT:] = w11
        att[CUT:, col] = nn(w10, v_h[:CUT]) + nn(w11, v_h[CUT:])
        return carry

    lax.fori_loop(0, HEADS // 2, inside, 0)
    scan_middle(0, False)
    lax.fori_loop(HEADS // 2, HEADS, inside, 0)
    scan_end(0, False, 1.0)

    def across(h, carry):
        col = columns(h)
        att[:, col] += nn(q8[:, col], scan[0, rows_of(h), :])
        return carry

    lax.fori_loop(0, HEADS, across, 0)

    def row_sums(b, carry):
        rows = pl.ds(pl.multiple_of(b * DH, DH), DH)
        squares = jnp.zeros((DH, DH), F32)
        inner = jnp.zeros((DH, DH), F32)
        for h in range(HEADS):
            col = slice(h * DH, (h + 1) * DH)
            a = att[rows, col]
            squares += a * a
            inner += a * (gain[:, col] * c[rows, col].astype(F32))
        stats[hx, 0:1, rows] = jnp.sum(squares.T, axis=0, keepdims=True)
        stats[hx, 1:2, rows] = jnp.sum(inner.T, axis=0, keepdims=True)
        return carry

    lax.fori_loop(0, TOK // DH, row_sums, 0)
    for step in range(1, NX):
        send(stats.at[hx], stats.at[hx], 8, (place, lax.rem(hx + step, NX)))
    await_bytes(stats.at[pl.ds(0, NX - 1)], recv_sem.at[8])
    sums = stats[0] + stats[1] + stats[2] + stats[3]
    mean_square = sums[0:1] * (1.0 / FULL_WIDTH) + 1e-6
    inverse = 1.0 / jnp.sqrt(mean_square)
    factor = sums[1:2] / (FULL_WIDTH * mean_square)
    for b in range(TOK // DH):
        rows = slice(b * DH, (b + 1) * DH)
        inv_ref[rows, :] = jnp.broadcast_to(inverse[:, rows], (DH, DH)).T
        fac_ref[rows, :] = jnp.broadcast_to(factor[:, rows], (DH, DH)).T

    def gradient_state(h):
        col = columns(h)
        scaled = gain[:, col] * c[:, col].astype(F32)
        g_h = ((scaled - att[:, col] * fac_ref[...]) * inv_ref[...]).astype(BF16)
        g[:, col] = g_h
        return tn(q[:, col], g_h)

    scan_begin(1, gradient_state, False)

    def inside_back(h, carry):
        col = columns(h)
        normed[:, col] = (gain[:, col] * att[:, col] * inv_ref[...]).astype(BF16)
        q_h, k_h, v_h, g_h = q[:, col], k[:, col], v[:, col], g[:, col]
        g8 = g_h * jnp.asarray(1.0 / DH, BF16)
        before = scan[0, rows_of(h), :]
        u00 = lower(nt(g8[:CUT], v_h[:CUT]))
        u10 = nt(g8[CUT:], v_h[:CUT]).astype(BF16)
        u11 = lower(nt(g8[CUT:], v_h[CUT:]))
        grad_q[:CUT, col] = (nn(u00, k_h[:CUT]) + nt(g8[:CUT], before)).astype(BF16)
        grad_q[CUT:, col] = (
            nn(u10, k_h[:CUT]) + nn(u11, k_h[CUT:]) + nt(g8[CUT:], before)
        ).astype(BF16)
        part_k[:CUT, col] = tn(u00, q_h[:CUT]) + tn(u10, q_h[CUT:])
        part_k[CUT:, col] = tn(u11, q_h[CUT:])
        part_v[:CUT, col] = tn(w[h, :CUT, :CUT], g_h[:CUT]) + tn(w[h, CUT:, :CUT], g_h[CUT:])
        part_v[CUT:, col] = tn(w[h, CUT:, CUT:], g_h[CUT:])
        return carry

    lax.fori_loop(0, HEADS // 2, inside_back, 0)
    scan_middle(1, True)
    lax.fori_loop(HEADS // 2, HEADS, inside_back, 0)
    scan_end(1, True, 1.0 / DH)

    suffix[...] = scan[1]

    for s in range(2):
        await_bytes(state_out.at[s], send_sem.at[4 * s])
        await_bytes(chip_sum.at[s, pl.ds(0, CHIPS - 1)], send_sem.at[4 * s + 1])
        await_bytes(scanned.at[s, pl.ds(0, CHIPS - 1)], send_sem.at[4 * s + 2])
        await_bytes(scan_out.at[s], send_sem.at[4 * s + 3])
    await_bytes(stats.at[pl.ds(0, NX - 1)], send_sem.at[8])


def finish(normed, grad_q, k, v, part_k, part_v, suffix, *rest):
    normed_out, grad_q_out, grad_k_out, grad_v_out, grad_k, grad_v, sem = rest
    stores = [
        pltpu.make_async_copy(normed, normed_out, sem.at[0]),
        pltpu.make_async_copy(grad_q, grad_q_out, sem.at[1]),
    ]
    for store in stores:
        store.start()
    for part in range(2):

        def last(i, carry):
            h = part * (HEADS // 2) + i
            col = pl.ds(pl.multiple_of(h * DH, DH), DH)
            after = suffix[col, :]
            grad_k[:, col] = (part_k[:, col] + nt(v[:, col], after)).astype(BF16)
            grad_v[:, col] = (part_v[:, col] + nn(k[:, col], after)).astype(BF16)
            return carry

        lax.fori_loop(0, HEADS // 2, last, 0)
        some = pl.ds(part * HALF, HALF)
        for n, (src, dst) in enumerate([(grad_k, grad_k_out), (grad_v, grad_v_out)]):
            store = pltpu.make_async_copy(src.at[:, some], dst.at[:, some], sem.at[2 + 2 * part + n])
            store.start()
            stores.append(store)
    for store in stores:
        store.wait()


def per_device(queries, key_rows, value_rows, norm_gain, cotangent):
    block = jax.ShapeDtypeStruct((TOK, WIDTH), BF16)
    held = pltpu.VMEM((TOK, WIDTH), BF16)
    held32 = pltpu.VMEM((TOK, WIDTH), F32)
    half = pltpu.VMEM((2, HALF, DH), BF16)
    pieces = pltpu.VMEM((2, CHIPS, PIECE, DH), BF16)
    passed = pl.pallas_call(
        kernel,
        out_shape=[held, held, held, held, held32, held32, pltpu.VMEM((WIDTH, DH), BF16)],
        in_specs=[pl.BlockSpec(memory_space=pltpu.HBM)] * 5,
        out_specs=[pl.BlockSpec(memory_space=pltpu.VMEM)] * 7,
        scratch_shapes=[
            held,
            pltpu.VMEM((1, WIDTH), F32),
            held,
            held,
            held,
            pltpu.VMEM((HEADS, TOK, TOK), BF16),
            held32,
            pltpu.VMEM((TOK, DH), F32),
            pltpu.VMEM((TOK, DH), F32),
            pltpu.VMEM((2, HALF, DH), F32),
            half,
            half,
            pieces,
            pieces,
            pieces,
            pieces,
            half,
            pltpu.VMEM((2, 2 * HALF, DH), BF16),
            pltpu.VMEM((NX, 2, TOK), F32),
            pltpu.SemaphoreType.DMA((5,)),
            pltpu.SemaphoreType.DMA((9,)),
            pltpu.SemaphoreType.DMA((9,)),
        ],
        compiler_params=pltpu.CompilerParams(
            collective_id=0, has_side_effects=True, vmem_limit_bytes=50 << 20
        ),
    )(queries, key_rows, value_rows, norm_gain.reshape(1, WIDTH), cotangent)
    return pl.pallas_call(
        finish,
        out_shape=[block] * 4,
        in_specs=[pl.BlockSpec(memory_space=pltpu.VMEM)] * 7,
        out_specs=[pl.BlockSpec(memory_space=pltpu.HBM)] * 4,
        scratch_shapes=[held, held, pltpu.SemaphoreType.DMA((6,))],
        compiler_params=pltpu.CompilerParams(vmem_limit_bytes=16 << 20),
    )(*passed)


def solution(mesh):
    placed = (P("ctx", "head"), P("ctx", "head"), P("ctx", "head"), P("head"), P("ctx", "head"))
    return jax.shard_map(
        per_device,
        mesh=mesh,
        in_specs=placed,
        out_specs=(P("ctx", "head"), P("ctx", "head"), P("ctx", "head"), P("ctx", "head")),
        check_vma=False,
    )
```

```python
import functools

import jax
import jax.numpy as jnp
from jax import lax
from jax.experimental import pallas as pl
from jax.experimental.pallas import tpu as pltpu
from jax.sharding import PartitionSpec as P

MESH = pl.DeviceIdType.MESH
F32 = jnp.float32
BF16 = jnp.bfloat16
DH = 128
TOK = 512
HEADS = 8
WIDTH = HEADS * DH
HALF = HEADS // 2 * DH
NY, NZ, NX = 4, 8, 4
CHIPS = NY * NZ
PIECE = HALF // CHIPS
FULL_WIDTH = WIDTH * NX
CUT = TOK // 2
FAR_REACH = 6
BLOCKS = 2
ROWS = TOK // BLOCKS


def far_first():
    def reach(offset):
        return min(offset[0], NY - offset[0]) + min(offset[1], NZ - offset[1])

    offsets = [(dy, dz) for dy in range(NY) for dz in range(NZ) if dy or dz]
    offsets = sorted(offsets, key=lambda offset: -reach(offset))
    far = [offset for offset in offsets if reach(offset) >= FAR_REACH]
    return far, offsets[len(far) :]


def nn(a, b):
    return lax.dot_general(a, b, (((1,), (0,)), ((), ())), preferred_element_type=F32)


def nt(a, b):
    return lax.dot_general(a, b, (((1,), (1,)), ((), ())), preferred_element_type=F32)


def tn(a, b):
    return lax.dot_general(a, b, (((0,), (0,)), ((), ())), preferred_element_type=F32)


def await_bytes(ref, sem):
    pltpu.make_async_copy(ref, ref, sem).wait()


def kernel(
    q_hbm,
    k_hbm,
    v_hbm,
    gain_hbm,
    c_hbm,
    normed,
    grad_q,
    grad_k,
    grad_v,
    k,
    v,
    part_k,
    part_v,
    suffix,
    q,
    gain,
    c,
    q8,
    q_turned,
    g,
    w,
    att,
    inv_ref,
    fac_ref,
    grad_state,
    state_own,
    state_out,
    state_in,
    chip_sum,
    owned,
    scanned,
    chip_scan,
    scan_out,
    scan,
    far_in,
    far_out,
    far_scan,
    stats,
    load_sem,
    send_sem,
    recv_sem,
):
    place = lax.axis_index("ctx")
    hx = lax.axis_index("head")
    chip = lax.div(place, 2)
    core = lax.rem(place, 2)
    chip_y = lax.div(chip, NZ)
    chip_z = lax.rem(chip, NZ)
    sibling = (chip * 2 + 1 - core, hx)

    def chip_at(dy, dz):
        return lax.rem(chip_y + dy, NY) * NZ + lax.rem(chip_z + dz, NZ)

    far, near = far_first()
    barrier = pltpu.get_barrier_semaphore()

    def greet(device):
        pl.semaphore_signal(barrier, inc=1, device_id=device, device_id_type=MESH)

    for dy, dz in far:
        greet((chip_at(dy, dz) * 2 + core, hx))
        greet((chip_at(dy, dz) * 2 + 1 - core, hx))
    for dy, dz in near:
        greet((chip_at(dy, dz) * 2 + core, hx))
    for step in range(1, NX):
        greet((place, lax.rem(hx + step, NX)))
    greet(sibling)
    greeted = 2 * len(far) + len(near) + NX

    loads = [
        pltpu.make_async_copy(src, dst, load_sem.at[n])
        for n, (src, dst) in enumerate(
            [(k_hbm, k), (v_hbm, v), (q_hbm, q), (gain_hbm, gain), (c_hbm, c)]
        )
    ]
    for load in loads:
        load.start()

    def columns(h):
        return pl.ds(pl.multiple_of(h * DH, DH), DH)

    def rows_of(h):
        return pl.ds(pl.multiple_of(h * DH, DH), DH)

    theirs = pl.multiple_of((1 - core) * HALF, HALF)
    ours = pl.multiple_of(core * HALF, HALF)

    def send(src, dst, n, device):
        pltpu.make_async_remote_copy(
            src_ref=src,
            dst_ref=dst,
            send_sem=send_sem.at[n],
            recv_sem=recv_sem.at[n],
            device_id=device,
            device_id_type=MESH,
        ).start()

    def scan_begin(s, local_state, first):
        def give(i, carry):
            state_out[s, 1 - core, rows_of(i), :] = local_state(
                (1 - core) * (HEADS // 2) + i
            ).astype(BF16)
            return carry

        def keep(i, carry):
            state = local_state(core * (HEADS // 2) + i)
            state_own[s, rows_of(i), :] = state
            state_out[s, core, rows_of(i), :] = state.astype(BF16)
            return carry

        lax.fori_loop(0, HEADS // 2, give, 0, unroll=True)
        if first:
            lax.fori_loop(0, HEADS // 2, keep, 0, unroll=True)
            pl.semaphore_wait(barrier, greeted)
        send(state_out.at[s, 1 - core], state_in.at[s], 6 * s, sibling)
        if not first:
            lax.fori_loop(0, HEADS // 2, keep, 0, unroll=True)
        for j, (dy, dz) in enumerate(far):
            other = chip_at(dy, dz)
            piece = pl.ds(pl.multiple_of(other * PIECE, PIECE), PIECE)
            for half in range(2):
                send(
                    state_out.at[s, half, piece],
                    far_in.at[s, j, core],
                    6 * s + 4,
                    (other * 2 + half, hx),
                )
        await_bytes(state_in.at[s], recv_sem.at[6 * s])
        both = state_own[s] + state_in[s].astype(F32)
        chip_sum[s] = both.astype(BF16).reshape(CHIPS, PIECE, DH)
        for dy, dz in near:
            other = chip_at(dy, dz)
            send(chip_sum.at[s, other], owned.at[s, chip], 6 * s + 1, (other * 2 + core, hx))
        owned[s, chip] = chip_sum[s, chip]
        for dy, dz in far:
            chip_scan[s, chip_at(dy, dz)] = jnp.zeros((PIECE, DH), BF16)

    def scan_middle(s, backward):
        leader = 1 if backward else 0
        await_bytes(far_in.at[s], recv_sem.at[6 * s + 4])
        for j, (dy, dz) in enumerate(far):
            both = far_in[s, j, 0].astype(F32) + far_in[s, j, 1].astype(F32)
            owned[s, chip_at(NY - dy, NZ - dz)] = both.astype(BF16)
        await_bytes(owned.at[s, pl.ds(0, len(near))], recv_sem.at[6 * s + 1])
        total = jnp.zeros((PIECE, DH), F32)
        for n in range(CHIPS):
            one = CHIPS - 1 - n if backward else n
            scanned[s, one] = total.astype(BF16)
            total = total + owned[s, one].astype(F32)
        for j, (dy, dz) in enumerate(far):
            other = chip_at(NY - dy, NZ - dz)
            ahead = scanned[s, other].astype(F32) + far_in[s, j, leader].astype(F32)
            far_out[s, j] = ahead.astype(BF16)
            for half in range(2):
                send(
                    scanned.at[s, other] if half == leader else far_out.at[s, j],
                    far_scan.at[s, j, core],
                    6 * s + 5,
                    (other * 2 + half, hx),
                )
        for dy, dz in near:
            other = chip_at(dy, dz)
            send(scanned.at[s, other], chip_scan.at[s, chip], 6 * s + 2, (other * 2 + core, hx))
        chip_scan[s, chip] = scanned[s, chip]

    def scan_end(s, backward, scale, own_half):
        await_bytes(chip_scan.at[s, pl.ds(0, len(near))], recv_sem.at[6 * s + 2])
        ahead = chip_scan[s].astype(F32).reshape(HALF, DH)
        leads = core == (1 if backward else 0)
        give = ahead + jnp.where(leads, state_own[s], 0.0)
        scan_out[s] = (give * scale).astype(BF16)
        send(scan_out.at[s], scan.at[s, pl.ds(ours, HALF)], 6 * s + 3, sibling)
        keep = ahead + jnp.where(leads, 0.0, state_in[s].astype(F32))
        scan[s, pl.ds(ours, HALF), :] = (keep * scale).astype(BF16)

        def place_far(half, base):
            for j, (dy, dz) in enumerate(far):
                at = pl.multiple_of(base + chip_at(dy, dz) * PIECE, PIECE)
                piece = far_scan[s, j, half].astype(F32) * scale
                scan[s, pl.ds(at, PIECE), :] = piece.astype(BF16)

        await_bytes(far_scan.at[s], recv_sem.at[6 * s + 5])
        place_far(core, ours)
        for i in range(HEADS // 2):
            own_half(i)
        await_bytes(scan_out.at[s], recv_sem.at[6 * s + 3])
        place_far(1 - core, theirs)

    row_at = lax.broadcasted_iota(jnp.int32, (CUT, CUT), 0)
    col_at = lax.broadcasted_iota(jnp.int32, (CUT, CUT), 1)
    causal = col_at <= row_at

    def lower(scores):
        return jnp.where(causal, scores, 0.0).astype(BF16)

    loads[0].wait()
    loads[1].wait()
    scan_begin(0, lambda h: tn(k[:, columns(h)], v[:, columns(h)]), True)
    for load in loads[2:]:
        load.wait()

    def inside(h, carry):
        col = columns(h)
        q8_h = q[:, col] * jnp.asarray(1.0 / DH, BF16)
        q8[:, col] = q8_h
        q_turned[rows_of(h), :] = q[:, col].T
        k_h, v_h = k[:, col], v[:, col]
        w00 = lower(nt(q8_h[:CUT], k_h[:CUT]))
        w[h, :CUT, :CUT] = w00
        att[:CUT, col] = nn(w00, v_h[:CUT])
        w10 = nt(q8_h[CUT:], k_h[:CUT]).astype(BF16)
        w11 = lower(nt(q8_h[CUT:], k_h[CUT:]))
        w[h, CUT:, :CUT] = w10
        w[h, CUT:, CUT:] = w11
        att[CUT:, col] = nn(w10, v_h[:CUT]) + nn(w11, v_h[CUT:])
        return carry

    lax.fori_loop(0, HEADS // 2, inside, 0)
    scan_middle(0, False)
    lax.fori_loop(HEADS // 2, HEADS, inside, 0)

    def across(rows, h):
        col = columns(h)
        att[rows, col] += nn(q8[rows, col], scan[0, rows_of(h), :])

    scan_end(0, False, 1.0, lambda i: across(slice(0, TOK), core * (HEADS // 2) + i))

    for b in range(BLOCKS):
        rows = slice(b * ROWS, (b + 1) * ROWS)
        for i in range(HEADS // 2):
            across(rows, (1 - core) * (HEADS // 2) + i)

        def row_sums(i, carry):
            at = pl.ds(pl.multiple_of(b * ROWS + i * DH, DH), DH)
            squares = jnp.zeros((DH, DH), F32)
            inner = jnp.zeros((DH, DH), F32)
            for h in range(HEADS):
                col = slice(h * DH, (h + 1) * DH)
                a = att[at, col]
                squares += a * a
                inner += a * (gain[:, col] * c[at, col].astype(F32))
            to = pl.ds(pl.multiple_of(i * DH, DH), DH)
            stats[b, hx, 0:1, to] = jnp.sum(squares.T, axis=0, keepdims=True)
            stats[b, hx, 1:2, to] = jnp.sum(inner.T, axis=0, keepdims=True)
            return carry

        lax.fori_loop(0, ROWS // DH, row_sums, 0, unroll=True)
        for step in range(1, NX):
            send(stats.at[b, hx], stats.at[b, hx], 12 + b, (place, lax.rem(hx + step, NX)))

    def gradient(b, h):
        rows = slice(b * ROWS, (b + 1) * ROWS)
        col = columns(h)
        scaled = gain[:, col] * c[rows, col].astype(F32)
        g_h = ((scaled - att[rows, col] * fac_ref[rows, :]) * inv_ref[rows, :]).astype(BF16)
        g[rows, col] = g_h
        return nn(q_turned[rows_of(h), rows], g_h)

    for b in range(BLOCKS):
        await_bytes(stats.at[b, pl.ds(0, NX - 1)], recv_sem.at[12 + b])
        sums = stats[b, 0] + stats[b, 1] + stats[b, 2] + stats[b, 3]
        mean_square = sums[0:1] * (1.0 / FULL_WIDTH) + 1e-6
        inverse = 1.0 / jnp.sqrt(mean_square)
        factor = sums[1:2] / (FULL_WIDTH * mean_square)
        for i in range(ROWS // DH):
            some = slice(i * DH, (i + 1) * DH)
            rows = slice(b * ROWS + i * DH, b * ROWS + (i + 1) * DH)
            inv_ref[rows, :] = jnp.broadcast_to(inverse[:, some], (DH, DH)).T
            fac_ref[rows, :] = jnp.broadcast_to(factor[:, some], (DH, DH)).T
        if b < BLOCKS - 1:
            for h in range(HEADS):
                state = gradient(b, h)
                grad_state[rows_of(h), :] = state if b == 0 else grad_state[rows_of(h), :] + state

    def gradient_state(h):
        return grad_state[rows_of(h), :] + gradient(BLOCKS - 1, h)

    scan_begin(1, gradient_state, False)

    def inside_back(h, carry):
        col = columns(h)
        normed[:, col] = (gain[:, col] * att[:, col] * inv_ref[...]).astype(BF16)
        q_h, k_h, v_h, g_h = q[:, col], k[:, col], v[:, col], g[:, col]
        g8 = g_h * jnp.asarray(1.0 / DH, BF16)
        before = scan[0, rows_of(h), :]
        u00 = lower(nt(g8[:CUT], v_h[:CUT]))
        u10 = nt(g8[CUT:], v_h[:CUT]).astype(BF16)
        u11 = lower(nt(g8[CUT:], v_h[CUT:]))
        grad_q[:CUT, col] = (nn(u00, k_h[:CUT]) + nt(g8[:CUT], before)).astype(BF16)
        grad_q[CUT:, col] = (
            nn(u10, k_h[:CUT]) + nn(u11, k_h[CUT:]) + nt(g8[CUT:], before)
        ).astype(BF16)
        part_k[:CUT, col] = tn(u00, q_h[:CUT]) + tn(u10, q_h[CUT:])
        part_k[CUT:, col] = tn(u11, q_h[CUT:])
        part_v[:CUT, col] = tn(w[h, :CUT, :CUT], g_h[:CUT]) + tn(w[h, CUT:, :CUT], g_h[CUT:])
        part_v[CUT:, col] = tn(w[h, CUT:, CUT:], g_h[CUT:])
        return carry

    lax.fori_loop(0, HEADS // 2, inside_back, 0)
    scan_middle(1, True)
    lax.fori_loop(HEADS // 2, HEADS, inside_back, 0)

    def finish_own(i):
        h = core * (HEADS // 2) + i
        col = columns(h)
        after = scan[1, rows_of(h), :]
        to = slice(i * DH, (i + 1) * DH)
        grad_k[:, to] = (part_k[:, col] + nt(v[:, col], after)).astype(BF16)
        grad_v[:, to] = (part_v[:, col] + nn(k[:, col], after)).astype(BF16)

    scan_end(1, True, 1.0 / DH, finish_own)

    suffix[...] = scan[1, pl.ds(theirs, HALF), :]

    for s in range(2):
        await_bytes(state_in.at[s], send_sem.at[6 * s])
        await_bytes(chip_sum.at[s, pl.ds(0, len(near))], send_sem.at[6 * s + 1])
        await_bytes(scanned.at[s, pl.ds(0, len(near))], send_sem.at[6 * s + 2])
        await_bytes(scan_out.at[s], send_sem.at[6 * s + 3])
        await_bytes(far_in.at[s], send_sem.at[6 * s + 4])
        await_bytes(far_scan.at[s], send_sem.at[6 * s + 5])
    for b in range(BLOCKS):
        await_bytes(stats.at[b, pl.ds(0, NX - 1)], send_sem.at[12 + b])


def finish(normed, grad_q, grad_k, grad_v, k, v, part_k, part_v, suffix, *rest):
    normed_out, grad_q_out, grad_k_out, grad_v_out, last_k, last_v, sem = rest
    core = lax.rem(lax.axis_index("ctx"), 2)
    ours = pl.ds(pl.multiple_of(core * HALF, HALF), HALF)
    stores = []

    def store(src, dst):
        copy = pltpu.make_async_copy(src, dst, sem.at[len(stores)])
        copy.start()
        stores.append(copy)

    store(normed, normed_out)
    store(grad_q, grad_q_out)
    store(grad_k, grad_k_out.at[:, ours])
    store(grad_v, grad_v_out.at[:, ours])
    for i in range(HEADS // 2):
        to = slice(i * DH, (i + 1) * DH)
        col = pl.ds(pl.multiple_of((1 - core) * HALF + i * DH, DH), DH)
        after = suffix[to, :]
        last_k[:, to] = (part_k[:, col] + nt(v[:, col], after)).astype(BF16)
        last_v[:, to] = (part_v[:, col] + nn(k[:, col], after)).astype(BF16)
        if i % 2:
            pair = pl.ds((i - 1) * DH, 2 * DH)
            out = pl.ds(pl.multiple_of((1 - core) * HALF + (i - 1) * DH, 2 * DH), 2 * DH)
            store(last_k.at[:, pair], grad_k_out.at[:, out])
            store(last_v.at[:, pair], grad_v_out.at[:, out])
    for copy in stores:
        copy.wait()


def per_device(queries, key_rows, value_rows, norm_gain, cotangent):
    block = jax.ShapeDtypeStruct((TOK, WIDTH), BF16)
    held = pltpu.VMEM((TOK, WIDTH), BF16)
    held32 = pltpu.VMEM((TOK, WIDTH), F32)
    held_half = pltpu.VMEM((TOK, HALF), BF16)
    suffix = pltpu.VMEM((HALF, DH), BF16)
    half = pltpu.VMEM((2, HALF, DH), BF16)
    pieces = pltpu.VMEM((2, CHIPS, PIECE, DH), BF16)
    far = len(far_first()[0])
    passed = pl.pallas_call(
        kernel,
        out_shape=[held, held, held_half, held_half, held, held, held32, held32, suffix],
        in_specs=[pl.BlockSpec(memory_space=pltpu.HBM)] * 5,
        out_specs=[pl.BlockSpec(memory_space=pltpu.VMEM)] * 9,
        scratch_shapes=[
            held,
            pltpu.VMEM((1, WIDTH), F32),
            held,
            held,
            pltpu.VMEM((WIDTH, TOK), BF16),
            held,
            pltpu.VMEM((HEADS, TOK, TOK), BF16),
            held32,
            pltpu.VMEM((TOK, DH), F32),
            pltpu.VMEM((TOK, DH), F32),
            pltpu.VMEM((WIDTH, DH), F32),
            pltpu.VMEM((2, HALF, DH), F32),
            pltpu.VMEM((2, 2, HALF, DH), BF16),
            half,
            pieces,
            pieces,
            pieces,
            pieces,
            half,
            pltpu.VMEM((2, 2 * HALF, DH), BF16),
            pltpu.VMEM((2, far, 2, PIECE, DH), BF16),
            pltpu.VMEM((2, far, PIECE, DH), BF16),
            pltpu.VMEM((2, far, 2, PIECE, DH), BF16),
            pltpu.VMEM((BLOCKS, NX, 2, ROWS), F32),
            pltpu.SemaphoreType.DMA((5,)),
            pltpu.SemaphoreType.DMA((12 + BLOCKS,)),
            pltpu.SemaphoreType.DMA((12 + BLOCKS,)),
        ],
        compiler_params=pltpu.CompilerParams(
            collective_id=0, has_side_effects=True, vmem_limit_bytes=50 << 20
        ),
    )(queries, key_rows, value_rows, norm_gain.reshape(1, WIDTH), cotangent)
    return pl.pallas_call(
        finish,
        out_shape=[block] * 4,
        in_specs=[pl.BlockSpec(memory_space=pltpu.VMEM)] * 9,
        out_specs=[pl.BlockSpec(memory_space=pltpu.HBM)] * 4,
        scratch_shapes=[held_half, held_half, pltpu.SemaphoreType.DMA((4 + HEADS // 2,))],
        compiler_params=pltpu.CompilerParams(vmem_limit_bytes=16 << 20),
    )(*passed)


def solution(mesh):
    placed = (P("ctx", "head"), P("ctx", "head"), P("ctx", "head"), P("head"), P("ctx", "head"))
    return jax.shard_map(
        per_device,
        mesh=mesh,
        in_specs=placed,
        out_specs=(P("ctx", "head"), P("ctx", "head"), P("ctx", "head"), P("ctx", "head")),
        check_vma=False,
    )
```

```python
import functools

import jax
import jax.numpy as jnp
from jax import lax
from jax.experimental import pallas as pl
from jax.experimental.pallas import tpu as pltpu
from jax.sharding import PartitionSpec as P

MESH = pl.DeviceIdType.MESH
F32 = jnp.float32
BF16 = jnp.bfloat16
DH = 128
TOK = 512
HEADS = 8
WIDTH = HEADS * DH
HALF = HEADS // 2 * DH
NY, NZ, NX = 4, 8, 4
CHIPS = NY * NZ
PIECE = HALF // CHIPS
FULL_WIDTH = WIDTH * NX
CUT = TOK // 2


def far_first():
    def reach(offset):
        return min(offset[0], NY - offset[0]) + min(offset[1], NZ - offset[1])

    offsets = [(dy, dz) for dy in range(NY) for dz in range(NZ) if dy or dz]
    return sorted(offsets, key=lambda offset: -reach(offset))


def nn(a, b):
    return lax.dot_general(a, b, (((1,), (0,)), ((), ())), preferred_element_type=F32)


def nt(a, b):
    return lax.dot_general(a, b, (((1,), (1,)), ((), ())), preferred_element_type=F32)


def tn(a, b):
    return lax.dot_general(a, b, (((0,), (0,)), ((), ())), preferred_element_type=F32)


def await_bytes(ref, sem):
    pltpu.make_async_copy(ref, ref, sem).wait()


def kernel(
    q_hbm,
    k_hbm,
    v_hbm,
    gain_hbm,
    c_hbm,
    normed,
    grad_q,
    grad_k,
    grad_v,
    k,
    v,
    part_k,
    part_v,
    suffix,
    q,
    kx,
    vx,
    c,
    gain,
    q8,
    q_turned,
    g,
    w,
    att,
    inv_ref,
    fac_ref,
    normed_out,
    grad_q_out,
    part_k_out,
    part_v_out,
    state_own,
    state_out,
    state_in,
    grad_state,
    chip_sum,
    owned,
    scanned,
    chip_scan,
    suffix_out,
    scan,
    stats,
    load_sem,
    send_sem,
    recv_sem,
):
    place = lax.axis_index("ctx")
    hx = lax.axis_index("head")
    chip = lax.div(place, 2)
    core = lax.rem(place, 2)
    chip_y = lax.div(chip, NZ)
    chip_z = lax.rem(chip, NZ)
    twin = chip * 2 + 1 - core
    sibling = (twin, hx)

    def chip_at(dy, dz):
        return lax.rem(chip_y + dy, NY) * NZ + lax.rem(chip_z + dz, NZ)

    offsets = far_first()
    barrier = pltpu.get_barrier_semaphore()

    def greet(device):
        pl.semaphore_signal(barrier, inc=1, device_id=device, device_id_type=MESH)

    for dy, dz in offsets:
        greet((chip_at(dy, dz) * 2 + core, hx))
    row = []
    for step in range(1, NX):
        row += [(place, lax.rem(hx + step, NX)), (twin, lax.rem(hx + step, NX))]
    row.append(sibling)
    for device in row:
        greet(device)

    ours = pl.ds(pl.multiple_of(core * HALF, HALF), HALF)
    theirs = pl.ds(pl.multiple_of((1 - core) * HALF, HALF), HALF)
    loads = [
        pltpu.make_async_copy(src, dst, load_sem.at[n])
        for n, (src, dst) in enumerate(
            [
                (k_hbm, k),
                (v_hbm, v),
                (q_hbm.at[:, ours], q.at[:, ours]),
                (k_hbm.at[:, ours], kx.at[:, ours]),
                (v_hbm.at[:, ours], vx.at[:, ours]),
                (c_hbm.at[:, ours], c.at[:, ours]),
                (gain_hbm.at[:, ours], gain.at[:, pl.ds(0, HALF)]),
                (gain_hbm.at[:, ours], gain.at[:, pl.ds(HALF, HALF)]),
            ]
        )
    ]
    for load in loads:
        load.start()

    def columns(h):
        return pl.ds(pl.multiple_of(h * DH, DH), DH)

    def send(src, dst, n, device):
        pltpu.make_async_remote_copy(
            src_ref=src,
            dst_ref=dst,
            send_sem=send_sem.at[n],
            recv_sem=recv_sem.at[n],
            device_id=device,
            device_id_type=MESH,
        ).start()

    def scan_begin(s, both):
        chip_sum[s] = both.astype(BF16).reshape(CHIPS, PIECE, DH)
        for dy, dz in offsets:
            other = chip_at(dy, dz)
            send(chip_sum.at[s, other], owned.at[s, chip], 2 * s, (other * 2 + core, hx))
        owned[s, chip] = chip_sum[s, chip]

    def scan_middle(s, backward):
        await_bytes(owned.at[s, pl.ds(0, CHIPS - 1)], recv_sem.at[2 * s])
        total = jnp.zeros((PIECE, DH), F32)
        for n in range(CHIPS):
            one = CHIPS - 1 - n if backward else n
            scanned[s, one] = total.astype(BF16)
            total = total + owned[s, one].astype(F32)
        for dy, dz in offsets:
            other = chip_at(dy, dz)
            send(scanned.at[s, other], chip_scan.at[s, chip], 2 * s + 1, (other * 2 + core, hx))
        chip_scan[s, chip] = scanned[s, chip]

    def scan_end(s):
        await_bytes(chip_scan.at[s, pl.ds(0, CHIPS - 1)], recv_sem.at[2 * s + 1])
        return chip_scan[s].astype(F32).reshape(HALF, DH)

    row_at = lax.broadcasted_iota(jnp.int32, (CUT, CUT), 0)
    col_at = lax.broadcasted_iota(jnp.int32, (CUT, CUT), 1)
    causal = col_at <= row_at

    def lower(scores):
        return jnp.where(causal, scores, 0.0).astype(BF16)

    loads[0].wait()
    loads[1].wait()
    for i in range(HEADS // 2):
        col = columns((1 - core) * (HEADS // 2) + i)
        state_out[columns(i), :] = tn(k[:, col], v[:, col]).astype(BF16)
    for i in range(HEADS // 2):
        col = columns(core * (HEADS // 2) + i)
        state_own[columns(i), :] = tn(k[:, col], v[:, col])
    pl.semaphore_wait(barrier, len(offsets) + len(row))
    send(state_out, state_in, 4, sibling)
    await_bytes(state_in, recv_sem.at[4])
    scan_begin(0, state_own[...] + state_in[...].astype(F32))
    shared = [(q_hbm, q), (k_hbm, kx), (v_hbm, vx), (c_hbm, c)]
    for n, (src, dst) in enumerate(shared):
        send(src.at[:, theirs], dst.at[:, ours], 8 + n, sibling)
    for load in loads[2:]:
        load.wait()

    def inside(h, carry):
        col = columns(h)
        q8_h = q[:, col] * jnp.asarray(1.0 / DH, BF16)
        q8[:, col] = q8_h
        q_turned[col, :] = q[:, col].T
        k_h, v_h = kx[:, col], vx[:, col]
        w00 = lower(nt(q8_h[:CUT], k_h[:CUT]))
        w[h, :CUT, :CUT] = w00
        att[:CUT, col] = nn(w00, v_h[:CUT])
        w10 = nt(q8_h[CUT:], k_h[:CUT]).astype(BF16)
        w11 = lower(nt(q8_h[CUT:], k_h[CUT:]))
        w[h, CUT:, :CUT] = w10
        w[h, CUT:, CUT:] = w11
        att[CUT:, col] = nn(w10, v_h[:CUT]) + nn(w11, v_h[CUT:])
        return carry

    first_own = core * (HEADS // 2)
    first_other = (1 - core) * (HEADS // 2)
    lax.fori_loop(first_own, first_own + HEADS // 2, inside, 0)
    scan_middle(0, False)
    for n, (src, dst) in enumerate(shared):
        await_bytes(dst.at[:, theirs], recv_sem.at[8 + n])
    lax.fori_loop(first_other, first_other + HEADS // 2, inside, 0)
    ahead = scan_end(0)
    scan[0, :HALF, :] = ahead.astype(BF16)
    between = jnp.where(core == 0, state_own[...], state_in[...].astype(F32))
    scan[0, HALF:, :] = (ahead + between).astype(BF16)

    slot = hx * 2 + core
    for b in range(2):
        for h in range(b * HEADS // 2, (b + 1) * HEADS // 2):
            col = slice(h * DH, (h + 1) * DH)
            att[:, col] += nn(q8[:, col], scan[0, col, :])
        for i in range(TOK // DH):
            rows = slice(i * DH, (i + 1) * DH)
            squares = jnp.zeros((DH, DH), F32)
            inner = jnp.zeros((DH, DH), F32)
            for h in range(b * HEADS // 2, (b + 1) * HEADS // 2):
                col = slice(h * DH, (h + 1) * DH)
                a = att[rows, col]
                squares += a * a
                inner += a * (gain[:, col] * c[rows, col].astype(F32))
            stats[b, slot, 0:1, rows] = jnp.sum(squares.T, axis=0, keepdims=True)
            stats[b, slot, 1:2, rows] = jnp.sum(inner.T, axis=0, keepdims=True)
        for device in row:
            send(stats.at[b, slot], stats.at[b, slot], 6 + b, device)

    for b in range(2):
        await_bytes(stats.at[b, pl.ds(0, len(row))], recv_sem.at[6 + b])
        sums = stats[b, 0]
        for n in range(1, len(row) + 1):
            sums = sums + stats[b, n]
        mean_square = sums[0:1] * (1.0 / FULL_WIDTH) + 1e-6
        inverse = 1.0 / jnp.sqrt(mean_square)
        factor = sums[1:2] / (FULL_WIDTH * mean_square)
        for i in range(TOK // DH):
            rows = slice(i * DH, (i + 1) * DH)
            inv_ref[b, rows, :] = jnp.broadcast_to(inverse[:, rows], (DH, DH)).T
            fac_ref[b, rows, :] = jnp.broadcast_to(factor[:, rows], (DH, DH)).T
        for h in range(b * HEADS // 2, (b + 1) * HEADS // 2):
            col = slice(h * DH, (h + 1) * DH)
            scaled = gain[:, col] * c[:, col].astype(F32)
            g_h = ((scaled - att[:, col] * fac_ref[b]) * inv_ref[b]).astype(BF16)
            g[:, col] = g_h
            grad_state[col, :] = nn(q_turned[col, :], g_h)
    scan_begin(1, grad_state[:HALF, :] + grad_state[HALF:, :])

    def inside_back(block, i, to_normed, to_q, to_k, to_v, to):
        h = block * (HEADS // 2) + i
        col = columns(h)
        inverse = inv_ref[block]
        to_normed[:, to] = (gain[:, col] * att[:, col] * inverse).astype(BF16)
        q_h, k_h, v_h, g_h = q[:, col], kx[:, col], vx[:, col], g[:, col]
        g8 = g_h * jnp.asarray(1.0 / DH, BF16)
        before = scan[0, col, :]
        u00 = lower(nt(g8[:CUT], v_h[:CUT]))
        u10 = nt(g8[CUT:], v_h[:CUT]).astype(BF16)
        u11 = lower(nt(g8[CUT:], v_h[CUT:]))
        to_q[:CUT, to] = (nn(u00, k_h[:CUT]) + nt(g8[:CUT], before)).astype(BF16)
        to_q[CUT:, to] = (
            nn(u10, k_h[:CUT]) + nn(u11, k_h[CUT:]) + nt(g8[CUT:], before)
        ).astype(BF16)
        to_k[:CUT, to] = tn(u00, q_h[:CUT]) + tn(u10, q_h[CUT:])
        to_k[CUT:, to] = tn(u11, q_h[CUT:])
        to_v[:CUT, to] = tn(w[h, :CUT, :CUT], g_h[:CUT]) + tn(w[h, CUT:, :CUT], g_h[CUT:])
        to_v[CUT:, to] = tn(w[h, CUT:, CUT:], g_h[CUT:])

    def for_sibling(i, carry):
        inside_back(1 - core, i, normed_out, grad_q_out, part_k_out, part_v_out, columns(i))
        return carry

    def for_own(i, carry):
        inside_back(core, i, normed, grad_q, part_k, part_v, columns(first_own + i))
        return carry

    lax.fori_loop(0, HEADS // 2, for_sibling, 0)
    send(normed_out, normed.at[:, ours], 12, sibling)
    send(grad_q_out, grad_q.at[:, ours], 13, sibling)
    scan_middle(1, True)
    send(part_k_out, part_k.at[:, ours], 14, sibling)
    send(part_v_out, part_v.at[:, ours], 15, sibling)
    lax.fori_loop(0, HEADS // 2, for_own, 0)
    ahead = scan_end(1)
    behind = ahead + grad_state[HALF:, :]
    suffix_out[...] = (jnp.where(core == 0, ahead, behind) * (1.0 / DH)).astype(BF16)
    send(suffix_out, suffix, 5, sibling)
    scan[1, :HALF, :] = (jnp.where(core == 0, behind, ahead) * (1.0 / DH)).astype(BF16)
    for i in range(HEADS // 2):
        col = columns(first_own + i)
        to = slice(i * DH, (i + 1) * DH)
        after = scan[1, to, :]
        grad_k[:, to] = (part_k[:, col] + nt(v[:, col], after)).astype(BF16)
        grad_v[:, to] = (part_v[:, col] + nn(k[:, col], after)).astype(BF16)

    staged = [(normed_out, normed), (grad_q_out, grad_q), (part_k_out, part_k), (part_v_out, part_v)]
    for n, (src, dst) in enumerate(staged):
        await_bytes(dst.at[:, theirs], recv_sem.at[12 + n])
        await_bytes(src, send_sem.at[12 + n])
    for s in range(2):
        await_bytes(chip_sum.at[s, pl.ds(0, CHIPS - 1)], send_sem.at[2 * s])
        await_bytes(scanned.at[s, pl.ds(0, CHIPS - 1)], send_sem.at[2 * s + 1])
    await_bytes(state_out, send_sem.at[4])
    for b in range(2):
        await_bytes(stats.at[b, pl.ds(0, len(row))], send_sem.at[6 + b])
    for n, (src, dst) in enumerate(shared):
        await_bytes(dst.at[:, theirs], send_sem.at[8 + n])
    await_bytes(suffix, recv_sem.at[5])
    await_bytes(suffix_out, send_sem.at[5])


def finish(normed, grad_q, grad_k, grad_v, k, v, part_k, part_v, suffix, *rest):
    normed_out, grad_q_out, grad_k_out, grad_v_out, last_k, last_v, sem = rest
    core = lax.rem(lax.axis_index("ctx"), 2)
    ours = pl.ds(pl.multiple_of(core * HALF, HALF), HALF)
    stores = []

    def store(src, dst):
        copy = pltpu.make_async_copy(src, dst, sem.at[len(stores)])
        copy.start()
        stores.append(copy)

    store(normed, normed_out)
    store(grad_q, grad_q_out)
    store(grad_k, grad_k_out.at[:, ours])
    store(grad_v, grad_v_out.at[:, ours])
    for i in range(HEADS // 2):
        to = slice(i * DH, (i + 1) * DH)
        col = pl.ds(pl.multiple_of((1 - core) * HALF + i * DH, DH), DH)
        after = suffix[to, :]
        last_k[:, to] = (part_k[:, col] + nt(v[:, col], after)).astype(BF16)
        last_v[:, to] = (part_v[:, col] + nn(k[:, col], after)).astype(BF16)
        if i % 2:
            pair = pl.ds((i - 1) * DH, 2 * DH)
            out = pl.ds(pl.multiple_of((1 - core) * HALF + (i - 1) * DH, 2 * DH), 2 * DH)
            store(last_k.at[:, pair], grad_k_out.at[:, out])
            store(last_v.at[:, pair], grad_v_out.at[:, out])
    for copy in stores:
        copy.wait()


def per_device(queries, key_rows, value_rows, norm_gain, cotangent):
    block = jax.ShapeDtypeStruct((TOK, WIDTH), BF16)
    held = pltpu.VMEM((TOK, WIDTH), BF16)
    held32 = pltpu.VMEM((TOK, WIDTH), F32)
    held_half = pltpu.VMEM((TOK, HALF), BF16)
    suffix = pltpu.VMEM((HALF, DH), BF16)
    pieces = pltpu.VMEM((2, CHIPS, PIECE, DH), BF16)
    passed = pl.pallas_call(
        kernel,
        out_shape=[held, held, held_half, held_half, held, held, held32, held32, suffix],
        in_specs=[pl.BlockSpec(memory_space=pltpu.HBM)] * 5,
        out_specs=[pl.BlockSpec(memory_space=pltpu.VMEM)] * 9,
        scratch_shapes=[
            held,
            held,
            held,
            held,
            pltpu.VMEM((1, WIDTH), F32),
            held,
            pltpu.VMEM((WIDTH, TOK), BF16),
            held,
            pltpu.VMEM((HEADS, TOK, TOK), BF16),
            held32,
            pltpu.VMEM((2, TOK, DH), F32),
            pltpu.VMEM((2, TOK, DH), F32),
            held_half,
            held_half,
            pltpu.VMEM((TOK, HALF), F32),
            pltpu.VMEM((TOK, HALF), F32),
            pltpu.VMEM((HALF, DH), F32),
            suffix,
            suffix,
            pltpu.VMEM((WIDTH, DH), F32),
            pieces,
            pieces,
            pieces,
            pieces,
            suffix,
            pltpu.VMEM((2, WIDTH, DH), BF16),
            pltpu.VMEM((2, 2 * NX, 2, TOK), F32),
            pltpu.SemaphoreType.DMA((8,)),
            pltpu.SemaphoreType.DMA((16,)),
            pltpu.SemaphoreType.DMA((16,)),
        ],
        compiler_params=pltpu.CompilerParams(
            collective_id=0, has_side_effects=True, vmem_limit_bytes=50 << 20
        ),
    )(queries, key_rows, value_rows, norm_gain.reshape(1, WIDTH), cotangent)
    return pl.pallas_call(
        finish,
        out_shape=[block] * 4,
        in_specs=[pl.BlockSpec(memory_space=pltpu.VMEM)] * 9,
        out_specs=[pl.BlockSpec(memory_space=pltpu.HBM)] * 4,
        scratch_shapes=[held_half, held_half, pltpu.SemaphoreType.DMA((4 + HEADS // 2,))],
        compiler_params=pltpu.CompilerParams(vmem_limit_bytes=16 << 20),
    )(*passed)


def solution(mesh):
    placed = (P("ctx", "head"), P("ctx", "head"), P("ctx", "head"), P("head"), P("ctx", "head"))
    return jax.shard_map(
        per_device,
        mesh=mesh,
        in_specs=placed,
        out_specs=(P("ctx", "head"), P("ctx", "head"), P("ctx", "head"), P("ctx", "head")),
        check_vma=False,
    )
```

```python
import functools

import jax
import jax.numpy as jnp
from jax import lax
from jax.experimental import pallas as pl
from jax.experimental.pallas import tpu as pltpu
from jax.sharding import PartitionSpec as P

MESH = pl.DeviceIdType.MESH
F32 = jnp.float32
BF16 = jnp.bfloat16
DH = 128
TOK = 512
HEADS = 8
WIDTH = HEADS * DH
HALF = HEADS // 2 * DH
NY, NZ, NX = 4, 8, 4
CHIPS = NY * NZ
PIECE = HALF // CHIPS
FULL_WIDTH = WIDTH * NX
CUT = TOK // 2


def far_first():
    def reach(offset):
        return min(offset[0], NY - offset[0]) + min(offset[1], NZ - offset[1])

    offsets = [(dy, dz) for dy in range(NY) for dz in range(NZ) if dy or dz]
    return sorted(offsets, key=lambda offset: -reach(offset))


def nn(a, b):
    return lax.dot_general(a, b, (((1,), (0,)), ((), ())), preferred_element_type=F32)


def nt(a, b):
    return lax.dot_general(a, b, (((1,), (1,)), ((), ())), preferred_element_type=F32)


def tn(a, b):
    return lax.dot_general(a, b, (((0,), (0,)), ((), ())), preferred_element_type=F32)


def await_bytes(ref, sem):
    pltpu.make_async_copy(ref, ref, sem).wait()


def kernel(
    q_hbm,
    k_hbm,
    v_hbm,
    gain_hbm,
    c_hbm,
    normed,
    grad_q,
    grad_k,
    grad_v,
    k,
    v,
    part_k,
    part_v,
    suffix,
    q,
    kx,
    vx,
    c,
    gain,
    q8,
    q_turned,
    g,
    w,
    att,
    inv_ref,
    fac_ref,
    normed_out,
    grad_q_out,
    part_k_out,
    part_v_out,
    state_own,
    state_out,
    state_in,
    grad_state,
    chip_sum,
    owned,
    scanned,
    chip_scan,
    suffix_out,
    scan,
    stats,
    load_sem,
    send_sem,
    recv_sem,
):
    place = lax.axis_index("ctx")
    hx = lax.axis_index("head")
    chip = lax.div(place, 2)
    core = lax.rem(place, 2)
    chip_y = lax.div(chip, NZ)
    chip_z = lax.rem(chip, NZ)
    twin = chip * 2 + 1 - core
    sign = 1 - 2 * core
    sibling = (twin, hx)

    def chip_at(dy, dz):
        y = lax.rem(chip_y + NY + sign * dy, NY)
        return y * NZ + lax.rem(chip_z + NZ + sign * dz, NZ)

    offsets = far_first()
    barrier = pltpu.get_barrier_semaphore()

    def greet(device):
        pl.semaphore_signal(barrier, inc=1, device_id=device, device_id_type=MESH)

    for dy, dz in offsets:
        greet((chip_at(dy, dz) * 2 + core, hx))
    row = []
    for step in (2, 1, 3):
        row += [(twin, lax.rem(hx + step, NX)), (place, lax.rem(hx + step, NX))]
    row.append(sibling)
    for device in row:
        greet(device)

    ours = pl.ds(pl.multiple_of(core * HALF, HALF), HALF)
    theirs = pl.ds(pl.multiple_of((1 - core) * HALF, HALF), HALF)
    loads = [
        pltpu.make_async_copy(src, dst, load_sem.at[n])
        for n, (src, dst) in enumerate(
            [
                (k_hbm.at[:, theirs], k.at[:, theirs]),
                (v_hbm.at[:, theirs], v.at[:, theirs]),
                (k_hbm.at[:, ours], k.at[:, ours]),
                (v_hbm.at[:, ours], v.at[:, ours]),
                (q_hbm.at[:, ours], q.at[:, ours]),
                (k_hbm.at[:, ours], kx.at[:, ours]),
                (v_hbm.at[:, ours], vx.at[:, ours]),
                (c_hbm.at[:, ours], c.at[:, ours]),
                (gain_hbm.at[:, ours], gain.at[:, pl.ds(0, HALF)]),
                (gain_hbm.at[:, ours], gain.at[:, pl.ds(HALF, HALF)]),
            ]
        )
    ]
    for load in loads[:4]:
        load.start()

    def columns(h):
        return pl.ds(pl.multiple_of(h * DH, DH), DH)

    def send(src, dst, n, device):
        pltpu.make_async_remote_copy(
            src_ref=src,
            dst_ref=dst,
            send_sem=send_sem.at[n],
            recv_sem=recv_sem.at[n],
            device_id=device,
            device_id_type=MESH,
        ).start()

    def scan_begin(s, both):
        chip_sum[s] = both.astype(BF16).reshape(CHIPS, PIECE, DH)
        for dy, dz in offsets:
            other = chip_at(dy, dz)
            send(chip_sum.at[s, other], owned.at[s, chip], 2 * s, (other * 2 + core, hx))
        owned[s, chip] = chip_sum[s, chip]

    def scan_middle(s, backward):
        await_bytes(owned.at[s, pl.ds(0, CHIPS - 1)], recv_sem.at[2 * s])
        total = jnp.zeros((PIECE, DH), F32)
        for n in range(CHIPS):
            one = CHIPS - 1 - n if backward else n
            scanned[s, one] = total.astype(BF16)
            total = total + owned[s, one].astype(F32)
        for dy, dz in offsets:
            other = chip_at(dy, dz)
            send(scanned.at[s, other], chip_scan.at[s, chip], 2 * s + 1, (other * 2 + core, hx))
        chip_scan[s, chip] = scanned[s, chip]

    def scan_end(s):
        await_bytes(chip_scan.at[s, pl.ds(0, CHIPS - 1)], recv_sem.at[2 * s + 1])
        return chip_scan[s].astype(F32).reshape(HALF, DH)

    row_at = lax.broadcasted_iota(jnp.int32, (CUT, CUT), 0)
    col_at = lax.broadcasted_iota(jnp.int32, (CUT, CUT), 1)
    causal = col_at <= row_at

    def lower(scores):
        return jnp.where(causal, scores, 0.0).astype(BF16)

    loads[0].wait()
    loads[1].wait()
    for i in range(HEADS // 2):
        col = columns((1 - core) * (HEADS // 2) + i)
        state_out[columns(i), :] = tn(k[:, col], v[:, col]).astype(BF16)
    loads[2].wait()
    loads[3].wait()
    for load in loads[4:]:
        load.start()
    for i in range(HEADS // 2):
        col = columns(core * (HEADS // 2) + i)
        state_own[columns(i), :] = tn(k[:, col], v[:, col])
    pl.semaphore_wait(barrier, len(offsets) + len(row))
    send(state_out, state_in, 4, sibling)
    await_bytes(state_in, recv_sem.at[4])
    scan_begin(0, state_own[...] + state_in[...].astype(F32))
    shared = [(q_hbm, q), (k_hbm, kx), (v_hbm, vx), (c_hbm, c)]
    for n, (src, dst) in enumerate(shared):
        send(src.at[:, theirs], dst.at[:, ours], 8 + n, sibling)
    for load in loads[4:]:
        load.wait()

    def inside(h, carry):
        col = columns(h)
        q8_h = q[:, col] * jnp.asarray(1.0 / DH, BF16)
        q8[:, col] = q8_h
        q_turned[col, :] = q[:, col].T
        k_h, v_h = kx[:, col], vx[:, col]
        w00 = lower(nt(q8_h[:CUT], k_h[:CUT]))
        w[h, :CUT, :CUT] = w00
        att[:CUT, col] = nn(w00, v_h[:CUT])
        w10 = nt(q8_h[CUT:], k_h[:CUT]).astype(BF16)
        w11 = lower(nt(q8_h[CUT:], k_h[CUT:]))
        w[h, CUT:, :CUT] = w10
        w[h, CUT:, CUT:] = w11
        att[CUT:, col] = nn(w10, v_h[:CUT]) + nn(w11, v_h[CUT:])
        return carry

    first_own = core * (HEADS // 2)
    first_other = (1 - core) * (HEADS // 2)
    lax.fori_loop(first_own, first_own + HEADS // 2, inside, 0)
    scan_middle(0, False)
    for n, (src, dst) in enumerate(shared):
        await_bytes(dst.at[:, theirs], recv_sem.at[8 + n])
    lax.fori_loop(first_other, first_other + HEADS // 2, inside, 0)
    ahead = scan_end(0)
    scan[0, :HALF, :] = ahead.astype(BF16)
    between = jnp.where(core == 0, state_own[...], state_in[...].astype(F32))
    scan[0, HALF:, :] = (ahead + between).astype(BF16)

    slot = hx * 2 + core
    for b in range(2):
        for h in range(b * HEADS // 2, (b + 1) * HEADS // 2):
            col = slice(h * DH, (h + 1) * DH)
            att[:, col] += nn(q8[:, col], scan[0, col, :])
        for i in range(TOK // DH):
            rows = slice(i * DH, (i + 1) * DH)
            squares = jnp.zeros((DH, DH), F32)
            inner = jnp.zeros((DH, DH), F32)
            for h in range(b * HEADS // 2, (b + 1) * HEADS // 2):
                col = slice(h * DH, (h + 1) * DH)
                a = att[rows, col]
                squares += a * a
                inner += a * (gain[:, col] * c[rows, col].astype(F32))
            stats[b, slot, 0:1, rows] = jnp.sum(squares.T, axis=0, keepdims=True)
            stats[b, slot, 1:2, rows] = jnp.sum(inner.T, axis=0, keepdims=True)
        for device in row:
            send(stats.at[b, slot], stats.at[b, slot], 6 + b, device)

    for b in range(2):
        await_bytes(stats.at[b, pl.ds(0, len(row))], recv_sem.at[6 + b])
        sums = stats[b, 0]
        for n in range(1, len(row) + 1):
            sums = sums + stats[b, n]
        mean_square = sums[0:1] * (1.0 / FULL_WIDTH) + 1e-6
        inverse = 1.0 / jnp.sqrt(mean_square)
        factor = sums[1:2] / (FULL_WIDTH * mean_square)
        for i in range(TOK // DH):
            rows = slice(i * DH, (i + 1) * DH)
            inv_ref[b, rows, :] = jnp.broadcast_to(inverse[:, rows], (DH, DH)).T
            fac_ref[b, rows, :] = jnp.broadcast_to(factor[:, rows], (DH, DH)).T
        for h in range(b * HEADS // 2, (b + 1) * HEADS // 2):
            col = slice(h * DH, (h + 1) * DH)
            scaled = gain[:, col] * c[:, col].astype(F32)
            g_h = ((scaled - att[:, col] * fac_ref[b]) * inv_ref[b]).astype(BF16)
            g[:, col] = g_h
            grad_state[col, :] = nn(q_turned[col, :], g_h)
    scan_begin(1, grad_state[:HALF, :] + grad_state[HALF:, :])

    def inside_back(block, i, to_normed, to_q, to_k, to_v, to):
        h = block * (HEADS // 2) + i
        col = columns(h)
        inverse = inv_ref[block]
        to_normed[:, to] = (gain[:, col] * att[:, col] * inverse).astype(BF16)
        q_h, k_h, v_h, g_h = q[:, col], kx[:, col], vx[:, col], g[:, col]
        g8 = g_h * jnp.asarray(1.0 / DH, BF16)
        before = scan[0, col, :]
        u00 = lower(nt(g8[:CUT], v_h[:CUT]))
        u10 = nt(g8[CUT:], v_h[:CUT]).astype(BF16)
        u11 = lower(nt(g8[CUT:], v_h[CUT:]))
        to_q[:CUT, to] = (nn(u00, k_h[:CUT]) + nt(g8[:CUT], before)).astype(BF16)
        to_q[CUT:, to] = (
            nn(u10, k_h[:CUT]) + nn(u11, k_h[CUT:]) + nt(g8[CUT:], before)
        ).astype(BF16)
        to_k[:CUT, to] = tn(u00, q_h[:CUT]) + tn(u10, q_h[CUT:])
        to_k[CUT:, to] = tn(u11, q_h[CUT:])
        to_v[:CUT, to] = tn(w[h, :CUT, :CUT], g_h[:CUT]) + tn(w[h, CUT:, :CUT], g_h[CUT:])
        to_v[CUT:, to] = tn(w[h, CUT:, CUT:], g_h[CUT:])

    def for_sibling(i, carry):
        inside_back(1 - core, i, normed_out, grad_q_out, part_k_out, part_v_out, columns(i))
        return carry

    def for_own(i, carry):
        inside_back(core, i, normed, grad_q, part_k, part_v, columns(first_own + i))
        return carry

    lax.fori_loop(0, HEADS // 2, for_sibling, 0)
    send(normed_out, normed.at[:, ours], 12, sibling)
    send(grad_q_out, grad_q.at[:, ours], 13, sibling)
    scan_middle(1, True)
    send(part_k_out, part_k.at[:, ours], 14, sibling)
    send(part_v_out, part_v.at[:, ours], 15, sibling)
    lax.fori_loop(0, HEADS // 2, for_own, 0)
    ahead = scan_end(1)
    behind = ahead + grad_state[HALF:, :]
    suffix_out[...] = (jnp.where(core == 0, ahead, behind) * (1.0 / DH)).astype(BF16)
    send(suffix_out, suffix, 5, sibling)
    scan[1, :HALF, :] = (jnp.where(core == 0, behind, ahead) * (1.0 / DH)).astype(BF16)
    for i in range(HEADS // 2):
        col = columns(first_own + i)
        to = slice(i * DH, (i + 1) * DH)
        after = scan[1, to, :]
        grad_k[:, to] = (part_k[:, col] + nt(v[:, col], after)).astype(BF16)
        grad_v[:, to] = (part_v[:, col] + nn(k[:, col], after)).astype(BF16)

    staged = [(normed_out, normed), (grad_q_out, grad_q), (part_k_out, part_k), (part_v_out, part_v)]
    for n, (src, dst) in enumerate(staged):
        await_bytes(dst.at[:, theirs], recv_sem.at[12 + n])
        await_bytes(src, send_sem.at[12 + n])
    for s in range(2):
        await_bytes(chip_sum.at[s, pl.ds(0, CHIPS - 1)], send_sem.at[2 * s])
        await_bytes(scanned.at[s, pl.ds(0, CHIPS - 1)], send_sem.at[2 * s + 1])
    await_bytes(state_out, send_sem.at[4])
    for b in range(2):
        await_bytes(stats.at[b, pl.ds(0, len(row))], send_sem.at[6 + b])
    for n, (src, dst) in enumerate(shared):
        await_bytes(dst.at[:, theirs], send_sem.at[8 + n])
    await_bytes(suffix, recv_sem.at[5])
    await_bytes(suffix_out, send_sem.at[5])


def finish(normed, grad_q, grad_k, grad_v, k, v, part_k, part_v, suffix, *rest):
    normed_out, grad_q_out, grad_k_out, grad_v_out, last_k, last_v, sem = rest
    core = lax.rem(lax.axis_index("ctx"), 2)
    ours = pl.ds(pl.multiple_of(core * HALF, HALF), HALF)
    stores = []

    def store(src, dst):
        copy = pltpu.make_async_copy(src, dst, sem.at[len(stores)])
        copy.start()
        stores.append(copy)

    store(normed, normed_out)
    store(grad_q, grad_q_out)
    store(grad_k, grad_k_out.at[:, ours])
    store(grad_v, grad_v_out.at[:, ours])
    for i in range(HEADS // 2):
        to = slice(i * DH, (i + 1) * DH)
        col = pl.ds(pl.multiple_of((1 - core) * HALF + i * DH, DH), DH)
        after = suffix[to, :]
        last_k[:, to] = (part_k[:, col] + nt(v[:, col], after)).astype(BF16)
        last_v[:, to] = (part_v[:, col] + nn(k[:, col], after)).astype(BF16)
        if i % 2:
            pair = pl.ds((i - 1) * DH, 2 * DH)
            out = pl.ds(pl.multiple_of((1 - core) * HALF + (i - 1) * DH, 2 * DH), 2 * DH)
            store(last_k.at[:, pair], grad_k_out.at[:, out])
            store(last_v.at[:, pair], grad_v_out.at[:, out])
    for copy in stores:
        copy.wait()


def per_device(queries, key_rows, value_rows, norm_gain, cotangent):
    block = jax.ShapeDtypeStruct((TOK, WIDTH), BF16)
    held = pltpu.VMEM((TOK, WIDTH), BF16)
    held32 = pltpu.VMEM((TOK, WIDTH), F32)
    held_half = pltpu.VMEM((TOK, HALF), BF16)
    suffix = pltpu.VMEM((HALF, DH), BF16)
    pieces = pltpu.VMEM((2, CHIPS, PIECE, DH), BF16)
    passed = pl.pallas_call(
        kernel,
        out_shape=[held, held, held_half, held_half, held, held, held32, held32, suffix],
        in_specs=[pl.BlockSpec(memory_space=pltpu.HBM)] * 5,
        out_specs=[pl.BlockSpec(memory_space=pltpu.VMEM)] * 9,
        scratch_shapes=[
            held,
            held,
            held,
            held,
            pltpu.VMEM((1, WIDTH), F32),
            held,
            pltpu.VMEM((WIDTH, TOK), BF16),
            held,
            pltpu.VMEM((HEADS, TOK, TOK), BF16),
            held32,
            pltpu.VMEM((2, TOK, DH), F32),
            pltpu.VMEM((2, TOK, DH), F32),
            held_half,
            held_half,
            pltpu.VMEM((TOK, HALF), F32),
            pltpu.VMEM((TOK, HALF), F32),
            pltpu.VMEM((HALF, DH), F32),
            suffix,
            suffix,
            pltpu.VMEM((WIDTH, DH), F32),
            pieces,
            pieces,
            pieces,
            pieces,
            suffix,
            pltpu.VMEM((2, WIDTH, DH), BF16),
            pltpu.VMEM((2, 2 * NX, 2, TOK), F32),
            pltpu.SemaphoreType.DMA((10,)),
            pltpu.SemaphoreType.DMA((16,)),
            pltpu.SemaphoreType.DMA((16,)),
        ],
        compiler_params=pltpu.CompilerParams(
            collective_id=0, has_side_effects=True, vmem_limit_bytes=50 << 20
        ),
    )(queries, key_rows, value_rows, norm_gain.reshape(1, WIDTH), cotangent)
    return pl.pallas_call(
        finish,
        out_shape=[block] * 4,
        in_specs=[pl.BlockSpec(memory_space=pltpu.VMEM)] * 9,
        out_specs=[pl.BlockSpec(memory_space=pltpu.HBM)] * 4,
        scratch_shapes=[held_half, held_half, pltpu.SemaphoreType.DMA((4 + HEADS // 2,))],
        compiler_params=pltpu.CompilerParams(vmem_limit_bytes=16 << 20),
    )(*passed)


def solution(mesh):
    placed = (P("ctx", "head"), P("ctx", "head"), P("ctx", "head"), P("head"), P("ctx", "head"))
    return jax.shard_map(
        per_device,
        mesh=mesh,
        in_specs=placed,
        out_specs=(P("ctx", "head"), P("ctx", "head"), P("ctx", "head"), P("ctx", "head")),
        check_vma=False,
    )
```

```python
import functools

import jax
import jax.numpy as jnp
from jax import lax
from jax.experimental import pallas as pl
from jax.experimental.pallas import tpu as pltpu
from jax.sharding import PartitionSpec as P

MESH = pl.DeviceIdType.MESH
F32 = jnp.float32
BF16 = jnp.bfloat16
DH = 128
TOK = 512
HEADS = 8
WIDTH = HEADS * DH
HALF = HEADS // 2 * DH
NY, NZ, NX = 4, 8, 4
CHIPS = NY * NZ
PIECE = HALF // CHIPS
FULL_WIDTH = WIDTH * NX
CUT = TOK // 2


def far_first():
    def reach(offset):
        return min(offset[0], NY - offset[0]) + min(offset[1], NZ - offset[1])

    offsets = [(dy, dz) for dy in range(NY) for dz in range(NZ) if dy or dz]
    return sorted(offsets, key=lambda offset: -reach(offset))


def nn(a, b):
    return lax.dot_general(a, b, (((1,), (0,)), ((), ())), preferred_element_type=F32)


def nt(a, b):
    return lax.dot_general(a, b, (((1,), (1,)), ((), ())), preferred_element_type=F32)


def tn(a, b):
    return lax.dot_general(a, b, (((0,), (0,)), ((), ())), preferred_element_type=F32)


def await_bytes(ref, sem):
    pltpu.make_async_copy(ref, ref, sem).wait()


def kernel(
    q_hbm,
    k_hbm,
    v_hbm,
    gain_hbm,
    c_hbm,
    normed,
    grad_q,
    grad_k,
    grad_v,
    k,
    v,
    part_k,
    part_v,
    suffix,
    q,
    kx,
    vx,
    c,
    gain,
    q8,
    q_turned,
    g,
    w,
    att,
    inv_ref,
    fac_ref,
    normed_out,
    grad_q_out,
    part_k_out,
    part_v_out,
    state_own,
    state_out,
    state_in,
    grad_state,
    chip_sum,
    owned,
    scanned,
    chip_scan,
    suffix_out,
    scan,
    paired,
    stats,
    load_sem,
    send_sem,
    recv_sem,
):
    place = lax.axis_index("ctx")
    hx = lax.axis_index("head")
    chip = lax.div(place, 2)
    core = lax.rem(place, 2)
    chip_y = lax.div(chip, NZ)
    chip_z = lax.rem(chip, NZ)
    twin = chip * 2 + 1 - core
    sign = 1 - 2 * core
    sibling = (twin, hx)

    ys = [lax.rem(chip_y + NY + sign * dy, NY) for dy in range(NY)]
    zs = [lax.rem(chip_z + NZ + sign * dz, NZ) for dz in range(NZ)]

    def chip_at(dy, dz):
        return ys[dy] * NZ + zs[dz]

    offsets = far_first()
    barrier = pltpu.get_barrier_semaphore()

    def greet(device):
        pl.semaphore_signal(barrier, inc=1, device_id=device, device_id_type=MESH)

    for dy, dz in offsets:
        greet((chip_at(dy, dz) * 2 + core, hx))
    row = []
    for step in (2, 1, 3):
        row += [(twin, lax.rem(hx + step, NX)), (place, lax.rem(hx + step, NX))]
    row.append(sibling)
    for device in row:
        greet(device)

    ours = pl.ds(pl.multiple_of(core * HALF, HALF), HALF)
    theirs = pl.ds(pl.multiple_of((1 - core) * HALF, HALF), HALF)
    loads = [
        pltpu.make_async_copy(src, dst, load_sem.at[n])
        for n, (src, dst) in enumerate(
            [
                (k_hbm.at[:, theirs], k.at[:, theirs]),
                (v_hbm.at[:, theirs], v.at[:, theirs]),
                (k_hbm.at[:, ours], k.at[:, ours]),
                (v_hbm.at[:, ours], v.at[:, ours]),
                (q_hbm.at[:, ours], q.at[:, ours]),
                (k_hbm.at[:, ours], kx.at[:, ours]),
                (v_hbm.at[:, ours], vx.at[:, ours]),
                (c_hbm.at[:, ours], c.at[:, ours]),
                (gain_hbm.at[:, ours], gain.at[:, pl.ds(0, HALF)]),
                (gain_hbm.at[:, ours], gain.at[:, pl.ds(HALF, HALF)]),
            ]
        )
    ]
    for load in loads[:4]:
        load.start()

    def columns(h):
        return pl.ds(pl.multiple_of(h * DH, DH), DH)

    def send(src, dst, n, device):
        pltpu.make_async_remote_copy(
            src_ref=src,
            dst_ref=dst,
            send_sem=send_sem.at[n],
            recv_sem=recv_sem.at[n],
            device_id=device,
            device_id_type=MESH,
        ).start()

    def scan_begin(s, both):
        chip_sum[s] = both.astype(BF16).reshape(CHIPS, PIECE, DH)
        for dy, dz in offsets:
            other = chip_at(dy, dz)
            send(chip_sum.at[s, other], owned.at[s, chip], 2 * s, (other * 2 + core, hx))
        owned[s, chip] = chip_sum[s, chip]

    def scan_middle(s, backward):
        await_bytes(owned.at[s, pl.ds(0, CHIPS - 1)], recv_sem.at[2 * s])
        total = jnp.zeros((PIECE, DH), F32)
        for n in range(CHIPS):
            one = CHIPS - 1 - n if backward else n
            scanned[s, one] = total.astype(BF16)
            total = total + owned[s, one].astype(F32)
        for dy, dz in offsets:
            other = chip_at(dy, dz)
            send(scanned.at[s, other], chip_scan.at[s, chip], 2 * s + 1, (other * 2 + core, hx))
        chip_scan[s, chip] = scanned[s, chip]

    def scan_end(s):
        await_bytes(chip_scan.at[s, pl.ds(0, CHIPS - 1)], recv_sem.at[2 * s + 1])
        return chip_scan[s].astype(F32).reshape(HALF, DH)

    row_at = lax.broadcasted_iota(jnp.int32, (CUT, CUT), 0)
    col_at = lax.broadcasted_iota(jnp.int32, (CUT, CUT), 1)
    causal = col_at <= row_at

    def lower(scores):
        return jnp.where(causal, scores, 0.0).astype(BF16)

    loads[0].wait()
    loads[1].wait()
    for i in range(HEADS // 2):
        col = columns((1 - core) * (HEADS // 2) + i)
        state_out[columns(i), :] = tn(k[:, col], v[:, col]).astype(BF16)
    loads[2].wait()
    loads[3].wait()
    for load in loads[4:]:
        load.start()
    for i in range(HEADS // 2):
        col = columns(core * (HEADS // 2) + i)
        state_own[columns(i), :] = tn(k[:, col], v[:, col])
    pl.semaphore_wait(barrier, len(offsets) + len(row))
    send(state_out, state_in, 4, sibling)
    await_bytes(state_in, recv_sem.at[4])
    scan_begin(0, state_own[...] + state_in[...].astype(F32))
    shared = [(q_hbm, q), (k_hbm, kx), (v_hbm, vx), (c_hbm, c)]
    for n, (src, dst) in enumerate(shared):
        send(src.at[:, theirs], dst.at[:, ours], 8 + n, sibling)
    for load in loads[4:]:
        load.wait()

    def inside(h, carry):
        col = columns(h)
        q8_h = q[:, col] * jnp.asarray(1.0 / DH, BF16)
        q8[:, col] = q8_h
        q_turned[col, :] = q[:, col].T
        k_h, v_h = kx[:, col], vx[:, col]
        w00 = lower(nt(q8_h[:CUT], k_h[:CUT]))
        w[h, :CUT, :CUT] = w00
        att[:CUT, col] = nn(w00, v_h[:CUT])
        w10 = nt(q8_h[CUT:], k_h[:CUT]).astype(BF16)
        w11 = lower(nt(q8_h[CUT:], k_h[CUT:]))
        w[h, CUT:, :CUT] = w10
        w[h, CUT:, CUT:] = w11
        att[CUT:, col] = nn(w10, v_h[:CUT]) + nn(w11, v_h[CUT:])
        return carry

    first_own = core * (HEADS // 2)
    first_other = (1 - core) * (HEADS // 2)
    lax.fori_loop(first_own, first_own + HEADS // 2, inside, 0)
    scan_middle(0, False)
    for n, (src, dst) in enumerate(shared):
        await_bytes(dst.at[:, theirs], recv_sem.at[8 + n])
    lax.fori_loop(first_other, first_other + HEADS // 2, inside, 0)
    paired[...] = jnp.zeros_like(paired)
    ahead = scan_end(0)
    scan[0, :HALF, :] = ahead.astype(BF16)
    between = jnp.where(core == 0, state_own[...], state_in[...].astype(F32))
    scan[0, HALF:, :] = (ahead + between).astype(BF16)
    for h in range(HEADS):
        side = slice(h % 2 * DH, (h % 2 + 1) * DH)
        paired[h // 2, side, side] = scan[0, h * DH : (h + 1) * DH, :]

    slot = hx * 2 + core
    for b in range(2):
        for pair in range(b * HEADS // 4, (b + 1) * HEADS // 4):
            col = slice(2 * pair * DH, (2 * pair + 2) * DH)
            att[:, col] += nn(q8[:, col], paired[pair])
        for i in range(TOK // DH):
            rows = slice(i * DH, (i + 1) * DH)
            squares = jnp.zeros((DH, DH), F32)
            inner = jnp.zeros((DH, DH), F32)
            for h in range(b * HEADS // 2, (b + 1) * HEADS // 2):
                col = slice(h * DH, (h + 1) * DH)
                a = att[rows, col]
                squares += a * a
                inner += a * (gain[:, col] * c[rows, col].astype(F32))
            stats[b, slot, 0:1, rows] = jnp.sum(squares.T, axis=0, keepdims=True)
            stats[b, slot, 1:2, rows] = jnp.sum(inner.T, axis=0, keepdims=True)
        for device in row:
            send(stats.at[b, slot], stats.at[b, slot], 6 + b, device)

    for b in range(2):
        await_bytes(stats.at[b, pl.ds(0, len(row))], recv_sem.at[6 + b])
        sums = stats[b, 0]
        for n in range(1, len(row) + 1):
            sums = sums + stats[b, n]
        mean_square = sums[0:1] * (1.0 / FULL_WIDTH) + 1e-6
        inverse = 1.0 / jnp.sqrt(mean_square)
        factor = sums[1:2] / (FULL_WIDTH * mean_square)
        for i in range(TOK // DH):
            rows = slice(i * DH, (i + 1) * DH)
            inv_ref[b, rows, :] = jnp.broadcast_to(inverse[:, rows], (DH, DH)).T
            fac_ref[b, rows, :] = jnp.broadcast_to(factor[:, rows], (DH, DH)).T
        for h in range(b * HEADS // 2, (b + 1) * HEADS // 2):
            col = slice(h * DH, (h + 1) * DH)
            scaled = gain[:, col] * c[:, col].astype(F32)
            g_h = ((scaled - att[:, col] * fac_ref[b]) * inv_ref[b]).astype(BF16)
            g[:, col] = g_h
            grad_state[col, :] = nn(q_turned[col, :], g_h)
    scan_begin(1, grad_state[:HALF, :] + grad_state[HALF:, :])

    def inside_back(block, i, to_normed, to_q, to_k, to_v, to):
        h = block * (HEADS // 2) + i
        col = columns(h)
        inverse = inv_ref[block]
        to_normed[:, to] = (gain[:, col] * att[:, col] * inverse).astype(BF16)
        q_h, k_h, v_h, g_h = q[:, col], kx[:, col], vx[:, col], g[:, col]
        g8 = g_h * jnp.asarray(1.0 / DH, BF16)
        before = scan[0, col, :]
        u00 = lower(nt(g8[:CUT], v_h[:CUT]))
        u10 = nt(g8[CUT:], v_h[:CUT]).astype(BF16)
        u11 = lower(nt(g8[CUT:], v_h[CUT:]))
        to_q[:CUT, to] = (nn(u00, k_h[:CUT]) + nt(g8[:CUT], before)).astype(BF16)
        to_q[CUT:, to] = (
            nn(u10, k_h[:CUT]) + nn(u11, k_h[CUT:]) + nt(g8[CUT:], before)
        ).astype(BF16)
        to_k[:CUT, to] = tn(u00, q_h[:CUT]) + tn(u10, q_h[CUT:])
        to_k[CUT:, to] = tn(u11, q_h[CUT:])
        to_v[:CUT, to] = tn(w[h, :CUT, :CUT], g_h[:CUT]) + tn(w[h, CUT:, :CUT], g_h[CUT:])
        to_v[CUT:, to] = tn(w[h, CUT:, CUT:], g_h[CUT:])

    def for_sibling(i, carry):
        inside_back(1 - core, i, normed_out, grad_q_out, part_k_out, part_v_out, columns(i))
        return carry

    def for_own(i, carry):
        inside_back(core, i, normed, grad_q, part_k, part_v, columns(first_own + i))
        return carry

    lax.fori_loop(0, HEADS // 2, for_sibling, 0)
    send(normed_out, normed.at[:, ours], 12, sibling)
    send(grad_q_out, grad_q.at[:, ours], 13, sibling)
    scan_middle(1, True)
    send(part_k_out, part_k.at[:, ours], 14, sibling)
    send(part_v_out, part_v.at[:, ours], 15, sibling)
    lax.fori_loop(0, HEADS // 2, for_own, 0)
    ahead = scan_end(1)
    behind = ahead + grad_state[HALF:, :]
    suffix_out[...] = (jnp.where(core == 0, ahead, behind) * (1.0 / DH)).astype(BF16)
    send(suffix_out, suffix, 5, sibling)
    scan[1, :HALF, :] = (jnp.where(core == 0, behind, ahead) * (1.0 / DH)).astype(BF16)
    for i in range(HEADS // 2):
        col = columns(first_own + i)
        to = slice(i * DH, (i + 1) * DH)
        after = scan[1, to, :]
        grad_k[:, to] = (part_k[:, col] + nt(v[:, col], after)).astype(BF16)
        grad_v[:, to] = (part_v[:, col] + nn(k[:, col], after)).astype(BF16)

    staged = [(normed_out, normed), (grad_q_out, grad_q), (part_k_out, part_k), (part_v_out, part_v)]
    for n, (src, dst) in enumerate(staged):
        await_bytes(dst.at[:, theirs], recv_sem.at[12 + n])
        await_bytes(src, send_sem.at[12 + n])
    for s in range(2):
        await_bytes(chip_sum.at[s, pl.ds(0, CHIPS - 1)], send_sem.at[2 * s])
        await_bytes(scanned.at[s, pl.ds(0, CHIPS - 1)], send_sem.at[2 * s + 1])
    await_bytes(state_out, send_sem.at[4])
    for b in range(2):
        await_bytes(stats.at[b, pl.ds(0, len(row))], send_sem.at[6 + b])
    for n, (src, dst) in enumerate(shared):
        await_bytes(dst.at[:, theirs], send_sem.at[8 + n])
    await_bytes(suffix, recv_sem.at[5])
    await_bytes(suffix_out, send_sem.at[5])


def finish(normed, grad_q, grad_k, grad_v, k, v, part_k, part_v, suffix, *rest):
    normed_out, grad_q_out, grad_k_out, grad_v_out, last_k, last_v, paired, sem = rest
    core = lax.rem(lax.axis_index("ctx"), 2)
    ours = pl.ds(pl.multiple_of(core * HALF, HALF), HALF)
    stores = []

    def store(src, dst):
        copy = pltpu.make_async_copy(src, dst, sem.at[len(stores)])
        copy.start()
        stores.append(copy)

    store(normed, normed_out)
    store(grad_q, grad_q_out)
    store(grad_k, grad_k_out.at[:, ours])
    store(grad_v, grad_v_out.at[:, ours])
    paired[...] = jnp.zeros_like(paired)
    for i in range(HEADS // 2):
        side = slice(i % 2 * DH, (i % 2 + 1) * DH)
        paired[i // 2, side, side] = suffix[i * DH : (i + 1) * DH, :]
    for i in range(HEADS // 4):
        pair = pl.ds(i * 2 * DH, 2 * DH)
        col = pl.ds(pl.multiple_of((1 - core) * HALF + i * 2 * DH, 2 * DH), 2 * DH)
        after = paired[i]
        last_k[:, pair] = (part_k[:, col] + nt(v[:, col], after)).astype(BF16)
        store(last_k.at[:, pair], grad_k_out.at[:, col])
        last_v[:, pair] = (part_v[:, col] + nn(k[:, col], after)).astype(BF16)
        store(last_v.at[:, pair], grad_v_out.at[:, col])
    for copy in stores:
        copy.wait()


def per_device(queries, key_rows, value_rows, norm_gain, cotangent):
    block = jax.ShapeDtypeStruct((TOK, WIDTH), BF16)
    held = pltpu.VMEM((TOK, WIDTH), BF16)
    held32 = pltpu.VMEM((TOK, WIDTH), F32)
    held_half = pltpu.VMEM((TOK, HALF), BF16)
    suffix = pltpu.VMEM((HALF, DH), BF16)
    pieces = pltpu.VMEM((2, CHIPS, PIECE, DH), BF16)
    passed = pl.pallas_call(
        kernel,
        out_shape=[held, held, held_half, held_half, held, held, held32, held32, suffix],
        in_specs=[pl.BlockSpec(memory_space=pltpu.HBM)] * 5,
        out_specs=[pl.BlockSpec(memory_space=pltpu.VMEM)] * 9,
        scratch_shapes=[
            held,
            held,
            held,
            held,
            pltpu.VMEM((1, WIDTH), F32),
            held,
            pltpu.VMEM((WIDTH, TOK), BF16),
            held,
            pltpu.VMEM((HEADS, TOK, TOK), BF16),
            held32,
            pltpu.VMEM((2, TOK, DH), F32),
            pltpu.VMEM((2, TOK, DH), F32),
            held_half,
            held_half,
            pltpu.VMEM((TOK, HALF), F32),
            pltpu.VMEM((TOK, HALF), F32),
            pltpu.VMEM((HALF, DH), F32),
            suffix,
            suffix,
            pltpu.VMEM((WIDTH, DH), F32),
            pieces,
            pieces,
            pieces,
            pieces,
            suffix,
            pltpu.VMEM((2, WIDTH, DH), BF16),
            pltpu.VMEM((HEADS // 2, 2 * DH, 2 * DH), BF16),
            pltpu.VMEM((2, 2 * NX, 2, TOK), F32),
            pltpu.SemaphoreType.DMA((10,)),
            pltpu.SemaphoreType.DMA((16,)),
            pltpu.SemaphoreType.DMA((16,)),
        ],
        compiler_params=pltpu.CompilerParams(
            collective_id=0, has_side_effects=True, vmem_limit_bytes=50 << 20
        ),
    )(queries, key_rows, value_rows, norm_gain.reshape(1, WIDTH), cotangent)
    return pl.pallas_call(
        finish,
        out_shape=[block] * 4,
        in_specs=[pl.BlockSpec(memory_space=pltpu.VMEM)] * 9,
        out_specs=[pl.BlockSpec(memory_space=pltpu.HBM)] * 4,
        scratch_shapes=[
            held_half,
            held_half,
            pltpu.VMEM((HEADS // 4, 2 * DH, 2 * DH), BF16),
            pltpu.SemaphoreType.DMA((4 + HEADS // 2,)),
        ],
        compiler_params=pltpu.CompilerParams(vmem_limit_bytes=16 << 20),
    )(*passed)


def solution(mesh):
    placed = (P("ctx", "head"), P("ctx", "head"), P("ctx", "head"), P("head"), P("ctx", "head"))
    return jax.shard_map(
        per_device,
        mesh=mesh,
        in_specs=placed,
        out_specs=(P("ctx", "head"), P("ctx", "head"), P("ctx", "head"), P("ctx", "head")),
        check_vma=False,
    )
```

```python
import functools

import jax
import jax.numpy as jnp
from jax import lax
from jax.experimental import pallas as pl
from jax.experimental.pallas import tpu as pltpu
from jax.sharding import PartitionSpec as P

MESH = pl.DeviceIdType.MESH
F32 = jnp.float32
BF16 = jnp.bfloat16
DH = 128
TOK = 512
HEADS = 8
WIDTH = HEADS * DH
HALF = HEADS // 2 * DH
NY, NZ, NX = 4, 8, 4
CHIPS = NY * NZ
PIECE = HALF // CHIPS
FULL_WIDTH = WIDTH * NX
CUT = TOK // 2
SPLIT = 2


def far_first():
    def reach(offset):
        return min(offset[0], NY - offset[0]) + min(offset[1], NZ - offset[1])

    offsets = [(dy, dz) for dy in range(NY) for dz in range(NZ) if dy or dz]
    return sorted(offsets, key=lambda offset: -reach(offset))


def nn(a, b):
    return lax.dot_general(a, b, (((1,), (0,)), ((), ())), preferred_element_type=F32)


def nt(a, b):
    return lax.dot_general(a, b, (((1,), (1,)), ((), ())), preferred_element_type=F32)


def tn(a, b):
    return lax.dot_general(a, b, (((0,), (0,)), ((), ())), preferred_element_type=F32)


def await_bytes(ref, sem):
    pltpu.make_async_copy(ref, ref, sem).wait()


def kernel(
    q_hbm,
    k_hbm,
    v_hbm,
    gain_hbm,
    c_hbm,
    normed,
    grad_q,
    grad_k,
    grad_v,
    k,
    v,
    part_k,
    part_v,
    suffix,
    q,
    kx,
    vx,
    c,
    gain,
    q8,
    q_turned,
    g,
    w,
    att,
    inv_ref,
    fac_ref,
    normed_out,
    grad_q_out,
    part_k_out,
    part_v_out,
    state_own,
    state_out,
    state_in,
    grad_state,
    chip_sum,
    owned,
    scanned,
    chip_scan,
    suffix_out,
    scan,
    stats,
    load_sem,
    send_sem,
    recv_sem,
):
    place = lax.axis_index("ctx")
    hx = lax.axis_index("head")
    chip = lax.div(place, 2)
    core = lax.rem(place, 2)
    chip_y = lax.div(chip, NZ)
    chip_z = lax.rem(chip, NZ)
    twin = chip * 2 + 1 - core
    sign = 1 - 2 * core
    sibling = (twin, hx)

    def chip_at(dy, dz):
        y = lax.rem(chip_y + NY + sign * dy, NY)
        return y * NZ + lax.rem(chip_z + NZ + sign * dz, NZ)

    offsets = far_first()
    barrier = pltpu.get_barrier_semaphore()

    def greet(device):
        pl.semaphore_signal(barrier, inc=1, device_id=device, device_id_type=MESH)

    for dy, dz in offsets:
        greet((chip_at(dy, dz) * 2 + core, hx))
    row = []
    for step in (2, 1, 3):
        row += [(twin, lax.rem(hx + step, NX)), (place, lax.rem(hx + step, NX))]
    row.append(sibling)
    for device in row:
        greet(device)

    ours = pl.ds(pl.multiple_of(core * HALF, HALF), HALF)
    theirs = pl.ds(pl.multiple_of((1 - core) * HALF, HALF), HALF)
    loads = [
        pltpu.make_async_copy(src, dst, load_sem.at[n])
        for n, (src, dst) in enumerate(
            [
                (k_hbm.at[:, theirs], k.at[:, theirs]),
                (v_hbm.at[:, theirs], v.at[:, theirs]),
                (k_hbm.at[:, ours], k.at[:, ours]),
                (v_hbm.at[:, ours], v.at[:, ours]),
                (q_hbm.at[:, ours], q.at[:, ours]),
                (k_hbm.at[:, ours], kx.at[:, ours]),
                (v_hbm.at[:, ours], vx.at[:, ours]),
                (c_hbm.at[:, ours], c.at[:, ours]),
                (gain_hbm.at[:, ours], gain.at[:, pl.ds(0, HALF)]),
                (gain_hbm.at[:, ours], gain.at[:, pl.ds(HALF, HALF)]),
            ]
        )
    ]
    for load in loads[:4]:
        load.start()

    def columns(h):
        return pl.ds(pl.multiple_of(h * DH, DH), DH)

    def send(src, dst, n, device):
        pltpu.make_async_remote_copy(
            src_ref=src,
            dst_ref=dst,
            send_sem=send_sem.at[n],
            recv_sem=recv_sem.at[n],
            device_id=device,
            device_id_type=MESH,
        ).start()

    def scan_begin(s, both):
        chip_sum[s] = both.astype(BF16).reshape(CHIPS, PIECE, DH)
        for dy, dz in offsets:
            other = chip_at(dy, dz)
            send(chip_sum.at[s, other], owned.at[s, chip], 2 * s, (other * 2 + core, hx))
        owned[s, chip] = chip_sum[s, chip]

    def scan_middle(s, backward):
        await_bytes(owned.at[s, pl.ds(0, CHIPS - 1)], recv_sem.at[2 * s])
        total = jnp.zeros((PIECE, DH), F32)
        for n in range(CHIPS):
            one = CHIPS - 1 - n if backward else n
            scanned[s, one] = total.astype(BF16)
            total = total + owned[s, one].astype(F32)
        for dy, dz in offsets:
            other = chip_at(dy, dz)
            send(scanned.at[s, other], chip_scan.at[s, chip], 2 * s + 1, (other * 2 + core, hx))
        chip_scan[s, chip] = scanned[s, chip]

    def scan_end(s):
        await_bytes(chip_scan.at[s, pl.ds(0, CHIPS - 1)], recv_sem.at[2 * s + 1])
        return chip_scan[s].astype(F32).reshape(HALF, DH)

    row_at = lax.broadcasted_iota(jnp.int32, (CUT, CUT), 0)
    col_at = lax.broadcasted_iota(jnp.int32, (CUT, CUT), 1)
    causal = col_at <= row_at

    def lower(scores):
        return jnp.where(causal, scores, 0.0).astype(BF16)

    loads[0].wait()
    loads[1].wait()
    for i in range(HEADS // 2):
        col = columns((1 - core) * (HEADS // 2) + i)
        state_out[columns(i), :] = tn(k[:, col], v[:, col]).astype(BF16)
    loads[2].wait()
    loads[3].wait()
    for load in loads[4:]:
        load.start()
    for i in range(HEADS // 2):
        col = columns(core * (HEADS // 2) + i)
        state_own[columns(i), :] = tn(k[:, col], v[:, col])
    pl.semaphore_wait(barrier, len(offsets) + len(row))
    send(state_out, state_in, 4, sibling)
    await_bytes(state_in, recv_sem.at[4])
    scan_begin(0, state_own[...] + state_in[...].astype(F32))
    shared = [(q_hbm, q), (k_hbm, kx), (v_hbm, vx), (c_hbm, c)]
    for n, (src, dst) in enumerate(shared):
        send(src.at[:, theirs], dst.at[:, ours], 8 + n, sibling)
    for load in loads[4:]:
        load.wait()

    def inside(h, carry):
        col = columns(h)
        q8_h = q[:, col] * jnp.asarray(1.0 / DH, BF16)
        q8[:, col] = q8_h
        q_turned[col, :] = q[:, col].T
        k_h, v_h = kx[:, col], vx[:, col]
        w00 = lower(nt(q8_h[:CUT], k_h[:CUT]))
        w[h, :CUT, :CUT] = w00
        att[:CUT, col] = nn(w00, v_h[:CUT])
        w10 = nt(q8_h[CUT:], k_h[:CUT]).astype(BF16)
        w11 = lower(nt(q8_h[CUT:], k_h[CUT:]))
        w[h, CUT:, :CUT] = w10
        w[h, CUT:, CUT:] = w11
        att[CUT:, col] = nn(w10, v_h[:CUT]) + nn(w11, v_h[CUT:])
        return carry

    first_own = core * (HEADS // 2)
    first_other = (1 - core) * (HEADS // 2)
    lax.fori_loop(first_own, first_own + HEADS // 2, inside, 0)
    scan_middle(0, False)
    for n, (src, dst) in enumerate(shared):
        await_bytes(dst.at[:, theirs], recv_sem.at[8 + n])
    lax.fori_loop(first_other, first_other + HEADS // 2, inside, 0)
    ahead = scan_end(0)
    scan[0, :HALF, :] = ahead.astype(BF16)
    between = jnp.where(core == 0, state_own[...], state_in[...].astype(F32))
    scan[0, HALF:, :] = (ahead + between).astype(BF16)

    slot = hx * 2 + core
    for b in range(2):
        for h in range(b * HEADS // 2, (b + 1) * HEADS // 2):
            col = slice(h * DH, (h + 1) * DH)
            att[:, col] += nn(q8[:, col], scan[0, col, :])
        for i in range(TOK // DH):
            rows = slice(i * DH, (i + 1) * DH)
            squares = jnp.zeros((DH, DH), F32)
            inner = jnp.zeros((DH, DH), F32)
            for h in range(b * HEADS // 2, (b + 1) * HEADS // 2):
                col = slice(h * DH, (h + 1) * DH)
                a = att[rows, col]
                squares += a * a
                inner += a * (gain[:, col] * c[rows, col].astype(F32))
            stats[b, slot, 0:1, rows] = jnp.sum(squares.T, axis=0, keepdims=True)
            stats[b, slot, 1:2, rows] = jnp.sum(inner.T, axis=0, keepdims=True)
        for device in row:
            send(stats.at[b, slot], stats.at[b, slot], 6 + b, device)

    for b in range(2):
        await_bytes(stats.at[b, pl.ds(0, len(row))], recv_sem.at[6 + b])
        sums = stats[b, 0]
        for n in range(1, len(row) + 1):
            sums = sums + stats[b, n]
        mean_square = sums[0:1] * (1.0 / FULL_WIDTH) + 1e-6
        inverse = 1.0 / jnp.sqrt(mean_square)
        factor = sums[1:2] / (FULL_WIDTH * mean_square)
        for i in range(TOK // DH):
            rows = slice(i * DH, (i + 1) * DH)
            inv_ref[b, rows, :] = jnp.broadcast_to(inverse[:, rows], (DH, DH)).T
            fac_ref[b, rows, :] = jnp.broadcast_to(factor[:, rows], (DH, DH)).T
        for h in range(b * HEADS // 2, (b + 1) * HEADS // 2):
            col = slice(h * DH, (h + 1) * DH)
            scaled = gain[:, col] * c[:, col].astype(F32)
            g_h = ((scaled - att[:, col] * fac_ref[b]) * inv_ref[b]).astype(BF16)
            g[:, col] = g_h
            grad_state[col, :] = nn(q_turned[col, :], g_h)
    scan_begin(1, grad_state[:HALF, :] + grad_state[HALF:, :])

    def inside_back(block, i, to_normed, to_q, to_k, to_v, to):
        h = block * (HEADS // 2) + i
        col = columns(h)
        inverse = inv_ref[block]
        to_normed[:, to] = (gain[:, col] * att[:, col] * inverse).astype(BF16)
        q_h, k_h, v_h, g_h = q[:, col], kx[:, col], vx[:, col], g[:, col]
        g8 = g_h * jnp.asarray(1.0 / DH, BF16)
        before = scan[0, col, :]
        u00 = lower(nt(g8[:CUT], v_h[:CUT]))
        u10 = nt(g8[CUT:], v_h[:CUT]).astype(BF16)
        u11 = lower(nt(g8[CUT:], v_h[CUT:]))
        to_q[:CUT, to] = (nn(u00, k_h[:CUT]) + nt(g8[:CUT], before)).astype(BF16)
        to_q[CUT:, to] = (
            nn(u10, k_h[:CUT]) + nn(u11, k_h[CUT:]) + nt(g8[CUT:], before)
        ).astype(BF16)
        to_k[:CUT, to] = tn(u00, q_h[:CUT]) + tn(u10, q_h[CUT:])
        to_k[CUT:, to] = tn(u11, q_h[CUT:])
        to_v[:CUT, to] = tn(w[h, :CUT, :CUT], g_h[:CUT]) + tn(w[h, CUT:, :CUT], g_h[CUT:])
        to_v[CUT:, to] = tn(w[h, CUT:, CUT:], g_h[CUT:])

    def for_sibling(i, carry):
        inside_back(1 - core, i, normed_out, grad_q_out, part_k_out, part_v_out, columns(i))
        return carry

    def for_own(i, carry):
        inside_back(core, i, normed, grad_q, part_k, part_v, columns(first_own + i))
        return carry

    lax.fori_loop(0, HEADS // 2, for_sibling, 0)
    send(normed_out, normed.at[:, ours], 12, sibling)
    send(grad_q_out, grad_q.at[:, ours], 13, sibling)
    scan_middle(1, True)
    send(part_k_out, part_k.at[:, ours], 14, sibling)
    send(part_v_out, part_v.at[:, ours], 15, sibling)
    lax.fori_loop(0, HEADS // 2, for_own, 0)
    ahead = scan_end(1)
    behind = ahead + grad_state[HALF:, :]
    suffix_out[...] = (jnp.where(core == 0, ahead, behind) * (1.0 / DH)).astype(BF16)
    send(suffix_out, suffix, 5, sibling)
    scan[1, :HALF, :] = (jnp.where(core == 0, behind, ahead) * (1.0 / DH)).astype(BF16)
    for i in range(HEADS // 2):
        col = columns(first_own + i)
        to = slice(i * DH, (i + 1) * DH)
        after = scan[1, to, :]
        grad_k[:, to] = (part_k[:, col] + nt(v[:, col], after)).astype(BF16)
        grad_v[:, to] = (part_v[:, col] + nn(k[:, col], after)).astype(BF16)

    staged = [(normed_out, normed), (grad_q_out, grad_q), (part_k_out, part_k), (part_v_out, part_v)]
    for n, (src, dst) in enumerate(staged):
        await_bytes(dst.at[:, theirs], recv_sem.at[12 + n])
        await_bytes(src, send_sem.at[12 + n])
    for s in range(2):
        await_bytes(chip_sum.at[s, pl.ds(0, CHIPS - 1)], send_sem.at[2 * s])
        await_bytes(scanned.at[s, pl.ds(0, CHIPS - 1)], send_sem.at[2 * s + 1])
    await_bytes(state_out, send_sem.at[4])
    for b in range(2):
        await_bytes(stats.at[b, pl.ds(0, len(row))], send_sem.at[6 + b])
    for n, (src, dst) in enumerate(shared):
        await_bytes(dst.at[:, theirs], send_sem.at[8 + n])
    await_bytes(suffix, recv_sem.at[5])
    await_bytes(suffix_out, send_sem.at[5])


def finish(normed, grad_q, grad_k, grad_v, k, v, part_k, part_v, suffix, *rest):
    normed_out, grad_q_out, grad_k_out, grad_v_out, last_k, last_v, sem = rest
    core = lax.rem(lax.axis_index("ctx"), 2)
    ours = pl.ds(pl.multiple_of(core * HALF, HALF), HALF)
    stores = []

    def store(src, dst):
        copy = pltpu.make_async_copy(src, dst, sem.at[len(stores)])
        copy.start()
        stores.append(copy)

    for part in range(SPLIT):
        rows = pl.ds(part * (TOK // SPLIT), TOK // SPLIT)
        store(normed.at[rows], normed_out.at[rows])
        store(grad_q.at[rows], grad_q_out.at[rows])
        store(grad_k.at[rows], grad_k_out.at[rows, ours])
        store(grad_v.at[rows], grad_v_out.at[rows, ours])
    for i in range(HEADS // 2):
        to = slice(i * DH, (i + 1) * DH)
        col = pl.ds(pl.multiple_of((1 - core) * HALF + i * DH, DH), DH)
        after = suffix[to, :]
        last_k[:, to] = (part_k[:, col] + nt(v[:, col], after)).astype(BF16)
        last_v[:, to] = (part_v[:, col] + nn(k[:, col], after)).astype(BF16)
        if i % 2:
            pair = pl.ds((i - 1) * DH, 2 * DH)
            out = pl.ds(pl.multiple_of((1 - core) * HALF + (i - 1) * DH, 2 * DH), 2 * DH)
            store(last_k.at[:, pair], grad_k_out.at[:, out])
            store(last_v.at[:, pair], grad_v_out.at[:, out])
    for copy in stores:
        copy.wait()


def per_device(queries, key_rows, value_rows, norm_gain, cotangent):
    block = jax.ShapeDtypeStruct((TOK, WIDTH), BF16)
    held = pltpu.VMEM((TOK, WIDTH), BF16)
    held32 = pltpu.VMEM((TOK, WIDTH), F32)
    held_half = pltpu.VMEM((TOK, HALF), BF16)
    suffix = pltpu.VMEM((HALF, DH), BF16)
    pieces = pltpu.VMEM((2, CHIPS, PIECE, DH), BF16)
    passed = pl.pallas_call(
        kernel,
        out_shape=[held, held, held_half, held_half, held, held, held32, held32, suffix],
        in_specs=[pl.BlockSpec(memory_space=pltpu.HBM)] * 5,
        out_specs=[pl.BlockSpec(memory_space=pltpu.VMEM)] * 9,
        scratch_shapes=[
            held,
            held,
            held,
            held,
            pltpu.VMEM((1, WIDTH), F32),
            held,
            pltpu.VMEM((WIDTH, TOK), BF16),
            held,
            pltpu.VMEM((HEADS, TOK, TOK), BF16),
            held32,
            pltpu.VMEM((2, TOK, DH), F32),
            pltpu.VMEM((2, TOK, DH), F32),
            held_half,
            held_half,
            pltpu.VMEM((TOK, HALF), F32),
            pltpu.VMEM((TOK, HALF), F32),
            pltpu.VMEM((HALF, DH), F32),
            suffix,
            suffix,
            pltpu.VMEM((WIDTH, DH), F32),
            pieces,
            pieces,
            pieces,
            pieces,
            suffix,
            pltpu.VMEM((2, WIDTH, DH), BF16),
            pltpu.VMEM((2, 2 * NX, 2, TOK), F32),
            pltpu.SemaphoreType.DMA((10,)),
            pltpu.SemaphoreType.DMA((16,)),
            pltpu.SemaphoreType.DMA((16,)),
        ],
        compiler_params=pltpu.CompilerParams(
            collective_id=0, has_side_effects=True, vmem_limit_bytes=50 << 20
        ),
    )(queries, key_rows, value_rows, norm_gain.reshape(1, WIDTH), cotangent)
    return pl.pallas_call(
        finish,
        out_shape=[block] * 4,
        in_specs=[pl.BlockSpec(memory_space=pltpu.VMEM)] * 9,
        out_specs=[pl.BlockSpec(memory_space=pltpu.HBM)] * 4,
        scratch_shapes=[held_half, held_half, pltpu.SemaphoreType.DMA((4 * SPLIT + HEADS // 2,))],
        compiler_params=pltpu.CompilerParams(vmem_limit_bytes=16 << 20),
    )(*passed)


def solution(mesh):
    placed = (P("ctx", "head"), P("ctx", "head"), P("ctx", "head"), P("head"), P("ctx", "head"))
    return jax.shard_map(
        per_device,
        mesh=mesh,
        in_specs=placed,
        out_specs=(P("ctx", "head"), P("ctx", "head"), P("ctx", "head"), P("ctx", "head")),
        check_vma=False,
    )
```
